128 devices in a mesh: rows: 8 (over z, core), cols: 16 (over x, y).
Axes of the slice: x: 4, y: 4, z: 4, core: 2. Of those that a mesh axis runs over, the one named last changes fastest.
Arguments:
- slip: float32 [4096, 2048], P('rows', 'cols'), may hold values from -6 to 6
- slip_rate: float32 [4096, 2048], P('rows', 'cols'), may hold values from -6 to 6
- loading: float32 [4096, 2048], P('rows', 'cols'), may hold values from -8 to 8
- friction: float32 [4096, 2048], P('rows', 'cols'), may hold values from 0.5 to 4
- state: float32 [4096, 2048], P('rows', 'cols'), may hold values from -1 to 1
- history: bfloat16 [32, 2, 2048, 4096], P(None, None, ('rows', 'cols')), may hold values from -6 to 6
- windows: int32 [2048, 4096], P(('rows', 'cols')), may hold values from 1 to 32, as said below
Outputs:
- velocity: float32 [4096, 2048], P('rows', 'cols')
- shear_stress: float32 [4096, 2048], P('rows', 'cols')
- rate_spectrum: float32 [2, 2048, 4096], P(None, ('rows', 'cols'))
The draws below stay inside these ranges and needn't reach their ends.
Inputs may be any that keep to these rules, and one draw needn't show every extreme that they name: windows[ky, kx] counts the stored spectra that mode (kx, ky) uses; mode (0, 0) uses all 32.
All inputs are finite; a program needn't handle non-finite values.
Results may differ from the reference program's by a relative error of at most 0.0003.
Values sent between devices are 32-bit elements; how exact they have to be, the bound alone decides.
No kernel may reach another device: no remote copies, remote signals or barrier semaphores. Data moves between devices by JAX's collectives and lax.ppermute only.
A program may use at most 64 MiB of HBM per device.

```python
import math
import jax
import jax.numpy as jnp
from jax import lax

NX = 4096
NY = 2048
HIST = 32
NEWTON = 3


def draw_windows(key, part):
    key = jax.random.fold_in(key, 7)
    ky_index = jnp.arange(NY, dtype=jnp.int32)[:, None]
    kx_index = jnp.arange(NX, dtype=jnp.int32)[None, :]
    fold_x = jnp.minimum(kx_index, NX - kx_index)
    fold_y = jnp.minimum(ky_index, NY - ky_index)
    baseline = HIST - fold_x * HIST // NX - fold_y * HIST // NY
    jitter = jax.random.randint(key, (NY, NX), -4, 1, dtype=jnp.int32)
    spread = jnp.clip(baseline + jitter, 1, HIST)
    return jnp.where(fold_x + fold_y == 0, HIST, spread).astype(jnp.int32)


def level_of(key, shape, pieces, low, top_value):
    def one(position, parts):
        steps = jax.random.uniform(jax.random.fold_in(jax.random.fold_in(key, 6), position), (parts,), jnp.float32, low / len(pieces), top_value / len(pieces))
        return jnp.repeat(jnp.exp(steps), shape[position] // parts).reshape((-1,) + (1,) * (len(shape) - position - 1))

    loudness = one(*pieces[0])
    for cut in pieces[1:]:
        loudness = loudness * one(*cut)
    return loudness


def bell_draw(rng, shape, scale, limit, shards=(), held_as=jnp.bfloat16):
    loudness = level_of(rng, shape, shards, -0.22, 0.18) if shards else 1.0
    array = jax.random.normal(rng, shape, jnp.float32) * scale * loudness
    return jnp.minimum(jnp.maximum(array, -limit), limit).astype(held_as)


def setup_inputs(seed: int = 0) -> dict:
    arg_keys = jax.random.split(jax.random.key(seed), 8)
    return {
        "slip": bell_draw(arg_keys[0], (NX, NY), 1.0, 6.0, ((0, 8), (1, 16)), jnp.float32),
        "slip_rate": bell_draw(arg_keys[1], (NX, NY), 1.0, 6.0, ((0, 8), (1, 16)), jnp.float32),
        "loading": bell_draw(arg_keys[2], (NX, NY), 2.0, 8.0, ((0, 8), (1, 16)), jnp.float32),
        "friction": jnp.clip(jnp.exp(math.log(4.0) - 2.0794415 * jax.random.uniform(arg_keys[3], (NX, NY), jnp.float32) ** level_of(arg_keys[3], (NX, NY), ((0, 8), (1, 16)), -0.2, 0.2)), 0.5, 4.0),
        "state": jnp.clip(jax.random.uniform(arg_keys[4], (NX, NY), jnp.float32, -1.0, 1.0) * level_of(arg_keys[4], (NX, NY), ((0, 8), (1, 16)), -0.4, 0.0), -1.0, 1.0),
        "history": bell_draw(arg_keys[5], (HIST, 2, NY, NX), 1.0, 6.0, ((2, 128),)),
        "windows": draw_windows(jax.random.fold_in(arg_keys[7], 71), 0),
    }


damping = 1.0

def inverse_sinh(value):
    absolute = jnp.abs(value)
    result = jnp.log(absolute + jnp.sqrt(1.0 + absolute * absolute))
    return jnp.where(value < 0, -result, result)

def magnitude(ky_index, kx_index):
    fold_x = jnp.minimum(kx_index, NX - kx_index).astype(jnp.float32) * (2.0 / NX)
    fold_y = jnp.minimum(ky_index, NY - ky_index).astype(jnp.float32) * (2.0 / NY)
    return jnp.sqrt(fold_x * fold_x + fold_y * fold_y)

def kernel(wavenumber, lag_value):
    taper = (2.0 * HIST + 2.0 - lag_value) / (2.0 * HIST + 2.0)
    return -0.5 * (wavenumber + 0.25) * jnp.cos(3.0 * lag_value * wavenumber) * taper

def reference(slip, slip_rate, loading, friction, state, history, windows):
    slip_hat = jnp.fft.fft2(slip, norm='ortho').T
    rate_hat = jnp.fft.fft2(slip_rate, norm='ortho').T
    ky_index = jnp.arange(NY, dtype=jnp.int32)[:, None]
    kx_index = jnp.arange(NX, dtype=jnp.int32)[None, :]
    wavenumber = magnitude(ky_index, kx_index)
    leading = kernel(wavenumber, jnp.float32(0.0))
    sum_real = -0.5 * wavenumber * jnp.real(slip_hat) + leading * jnp.real(rate_hat)
    sum_imag = -0.5 * wavenumber * jnp.imag(slip_hat) + leading * jnp.imag(rate_hat)

    def add_term(running, lag_index):
        stored = lax.dynamic_index_in_dim(history, lag_index - 1, 0, keepdims=False).astype(jnp.float32)
        weight = jnp.where(lag_index <= windows, kernel(wavenumber, lag_index.astype(jnp.float32)), 0.0)
        return ((running[0] + weight * stored[0], running[1] + weight * stored[1]), None)
    (sum_real, sum_imag), _ = lax.scan(add_term, (sum_real, sum_imag), jnp.arange(1, HIST + 1, dtype=jnp.int32))
    functional = (sum_real + 1j * sum_imag).T
    transfer = jnp.real(jnp.fft.ifft2(functional, norm='ortho')).astype(jnp.float32)
    traction = loading + transfer
    half_gain = 0.5 * jnp.exp(state)
    velocity = slip_rate
    for sweep in range(NEWTON):
        scaled = velocity * half_gain
        mismatch = friction * inverse_sinh(scaled) + damping * velocity - traction
        tangent = friction * half_gain / jnp.sqrt(1.0 + scaled * scaled) + damping
        velocity = velocity - mismatch / tangent
    spectrum = jnp.stack((jnp.real(rate_hat), jnp.imag(rate_hat))).astype(jnp.float32)
    return (velocity, traction - damping * velocity, spectrum)
```

```python
import functools
import math

import jax
import jax.numpy as jnp
import ml_dtypes
import numpy as np
from jax import lax
from jax.experimental import pallas as pl
from jax.experimental.pallas import tpu as pltpu
from jax.sharding import PartitionSpec as P

NX = 4096
NY = 2048
HIST = 32
NEWTON = 3
damping = 1.0
LANES = 512
VMEM_LIMIT = 24 * 1024 * 1024


def split_host(matrix):
    full = matrix.astype(np.float32)
    high = full.astype(ml_dtypes.bfloat16)
    low = (full - high.astype(np.float32)).astype(ml_dtypes.bfloat16)
    return np.stack((high, low))


def dft_matrix(sign, scale, transposed):
    index = np.arange(128)
    phase = sign * 2.0 * math.pi * (np.outer(index, index) % 128) / 128.0
    cos, sin = np.cos(phase) * scale, np.sin(phase) * scale
    matrix = np.block([[cos, sin], [-sin, cos]])
    return split_host(matrix.T if transposed else matrix)


def twiddle(count, length, sign):
    phase = sign * 2.0 * math.pi * np.outer(np.arange(count), np.arange(128)) / length
    return np.stack((np.cos(phase), np.sin(phase))).astype(np.float32)


def add(a, b):
    return (a[0] + b[0], a[1] + b[1])


def sub(a, b):
    return (a[0] - b[0], a[1] - b[1])


def conj(a):
    return (a[0], -a[1])


def turn(value, numerator, length, sign):
    numerator %= length
    re, im = value
    if numerator == 0:
        return value
    if 4 * numerator == length:
        return (-im, re) if sign > 0 else (im, -re)
    if 2 * numerator == length:
        return (-re, -im)
    if 4 * numerator == 3 * length:
        return (im, -re) if sign > 0 else (-im, re)
    if 8 * numerator % length == 0:
        half = math.sqrt(0.5)
        octant = 8 * numerator // length
        cos_sign = 1.0 if octant in (1, 7) else -1.0
        sin_sign = (1.0 if octant in (1, 3) else -1.0) * sign
        first = re if cos_sign > 0 else -re
        second = im if cos_sign > 0 else -im
        if sin_sign > 0:
            return ((first - im) * half, (re + second) * half)
        return ((first + im) * half, (second - re) * half)
    angle = 2.0 * math.pi * numerator / length
    cos, sin = math.cos(angle), sign * math.sin(angle)
    return (re * cos - im * sin, re * sin + im * cos)


def butterfly(values, sign):
    size = len(values)
    if size == 1:
        return values
    even = butterfly(values[0::2], sign)
    odd = butterfly(values[1::2], sign)
    turned = [turn(odd[k], k, size, sign) for k in range(size // 2)]
    return [add(e, t) for e, t in zip(even, turned)] + [sub(e, t) for e, t in zip(even, turned)]


def real_forward(values):
    size = len(values)
    if size == 2:
        return [(values[0] + values[1], None), (values[0] - values[1], None)]
    even = real_forward(values[0::2])
    odd = real_forward(values[1::2])
    quarter = size // 4
    out = [None] * (size // 2 + 1)
    for k in range(quarter + 1):
        e, o = even[k], odd[k]
        if k == 0:
            out[0] = (e[0] + o[0], None)
            out[size // 2] = (e[0] - o[0], None)
        elif k == quarter:
            out[k] = (e[0], -o[0])
        else:
            t = turn(o, k, size, -1)
            out[k] = add(e, t)
            out[size // 2 - k] = conj(sub(e, t))
    return out


def real_inverse(modes):
    half = len(modes) - 1
    size = 2 * half
    if size == 2:
        return [modes[0][0] + modes[1][0], modes[0][0] - modes[1][0]]
    quarter = half // 2
    even, odd = [], []
    for k in range(quarter + 1):
        a, b = modes[k], modes[half - k]
        if k == 0:
            even.append((a[0] + b[0], None))
            odd.append((a[0] - b[0], None))
        elif k == quarter:
            even.append((a[0] + a[0], None))
            odd.append((-(a[1] + a[1]), None))
        else:
            even.append(add(a, conj(b)))
            odd.append(turn(sub(a, conj(b)), k, size, 1))
    first, second = real_inverse(even), real_inverse(odd)
    out = []
    for e, o in zip(first, second):
        out += [e, o]
    return out


def times(value, table, index, rows=None):
    cos, sin = table[0, index : index + 1, :], table[1, index : index + 1, :]
    re, im = value
    if im is None:
        return (re * cos, re * sin)
    return (re * cos - im * sin, re * sin + im * cos)


def split(value):
    high = value.astype(jnp.bfloat16)
    return high, (value - high.astype(jnp.float32)).astype(jnp.bfloat16)


def dot(left, right, contract):
    return lax.dot_general(
        left, right, ((contract[0], contract[1]), ((), ())), preferred_element_type=jnp.float32
    )


def exact_dot(left, right, contract):
    (lh, ll), (rh, rl) = left, right
    return dot(lh, rh, contract) + (dot(lh, rl, contract) + dot(ll, rh, contract))


def lines_kernel(cells, table, matrix, out, work):
    for f in range(2):
        for group in range(4):
            samples = [cells[c, f, 8 * group : 8 * group + 8, :] for c in range(16)]
            modes = real_forward(samples)
            for k in range(16):
                if k <= 8:
                    value = modes[k]
                else:
                    value = conj(modes[16 - k])
                re, im = times(value, table, k)
                rows = pl.ds(8 * group * 32 + f * 16 + k, 8, stride=32)
                work[0, rows, :] = re
                work[1, rows, :] = im
    weights = (matrix[0], matrix[1])
    for chunk in range(4):
        rows = pl.ds(chunk * 256, 256)
        turned = jnp.concatenate((work[0, rows, :], work[1, rows, :]), axis=1)
        result = exact_dot(weights, split(turned), ((1,), (1,)))
        for part in range(2):
            for piece in range(2):
                out[pl.ds(part * 8 + chunk * 2 + piece, 128, stride=16), :] = result[
                    part * 128 : part * 128 + 128, piece * 128 : piece * 128 + 128
                ]


def history_kernel(first_ky, stored, windows, total, waves):
    block = pl.program_id(0)
    step = 256
    for piece in range(LANES // step):
        lanes = pl.ds(piece * step, step)
        shape = (16, step)
        ky = lax.broadcasted_iota(jnp.int32, shape, 0) + first_ky[0]
        kx = lax.broadcasted_iota(jnp.int32, shape, 1) + (block * LANES + piece * step)
        fold_x = jnp.minimum(kx, NX - kx).astype(jnp.float32) * (2.0 / NX)
        fold_y = jnp.minimum(ky, NY - ky).astype(jnp.float32) * (2.0 / NY)
        wave = jnp.sqrt(fold_x * fold_x + fold_y * fold_y)
        waves[:, lanes] = wave
        count = windows[:, lanes]
        current = jnp.cos(3.0 * wave)
        double = current + current
        previous = None
        real = jnp.zeros(shape, jnp.float32)
        imag = jnp.zeros(shape, jnp.float32)
        for lag in range(1, HIST + 1):
            if lag == 2:
                previous, current = current, double * current - 1.0
            elif lag > 2:
                previous, current = current, double * current - previous
            weight = jnp.where(count >= lag, current * (2.0 * HIST + 2.0 - lag), 0.0)
            real = real + weight * stored[lag - 1, 0, :, lanes].astype(jnp.float32)
            imag = imag + weight * stored[lag - 1, 1, :, lanes].astype(jnp.float32)
        factor = (wave + 0.25) * (-0.5 / (2.0 * HIST + 2.0))
        total[0, :, lanes] = factor * real
        total[1, :, lanes] = factor * imag


def modes_kernel(
    arrived, summed, waves, turn_in, turn_out, into, back, spectrum, out, left, mid, spec, gathered, turned
):
    for piece in range(8):
        for part in range(2):
            tile = arrived[pl.ds(part * 8 + piece, 128, stride=16), :]
            left[piece * 128 : piece * 128 + 128, part * 128 : part * 128 + 128] = tile.T
    weights = (into[0], into[1])
    for piece in range(4):
        rows = pl.ds(piece * 256, 256)
        mid[rows, :] = exact_dot(split(left[rows, :]), weights, ((1,), (0,)))
    for f in range(2):
        for half in range(2):
            first = f * 16 + half * 8
            for i1 in range(4):
                values = []
                for i2 in range(8):
                    i = i1 + 4 * i2
                    row = i * 32 + first
                    value = (mid[row : row + 8, 0:128], mid[row : row + 8, 128:256])
                    values.append(times(value, turn_in, i))
                for b1, value in enumerate(butterfly(values, -1)):
                    value = turn(value, i1 * b1, 32, -1)
                    spec[0, i1 * 8 + b1] = value[0]
                    spec[1, i1 * 8 + b1] = value[1]
            for b1 in range(8):
                values = [(spec[0, i1 * 8 + b1], spec[1, i1 * 8 + b1]) for i1 in range(4)]
                for b2, value in enumerate(butterfly(values, -1)):
                    b = b1 + 8 * b2
                    for part in range(2):
                        rows = slice(half * 8, half * 8 + 8)
                        lanes = slice(b * 128, b * 128 + 128)
                        if f == 1:
                            spectrum[part, rows, lanes] = value[part]
                        else:
                            gathered[part, rows, lanes] = value[part]
    for half in range(2):
        rows = slice(half * 8, half * 8 + 8)
        for b1 in range(8):
            values = []
            for b2 in range(4):
                b = b1 + 8 * b2
                lanes = slice(b * 128, b * 128 + 128)
                wave = waves[rows, lanes]
                slip_weight = -0.5 * wave
                rate_weight = -0.5 * (wave + 0.25)
                values.append(
                    tuple(
                        slip_weight * gathered[part, rows, lanes]
                        + rate_weight * spectrum[part, rows, lanes]
                        + summed[part, rows, lanes]
                        for part in range(2)
                    )
                )
            for i1, value in enumerate(butterfly(values, 1)):
                value = turn(value, i1 * b1, 32, 1)
                spec[0, i1 * 8 + b1] = value[0]
                spec[1, i1 * 8 + b1] = value[1]
        for i1 in range(4):
            values = [(spec[0, i1 * 8 + b1], spec[1, i1 * 8 + b1]) for b1 in range(8)]
            for i2, value in enumerate(butterfly(values, 1)):
                i = i1 + 4 * i2
                value = times(value, turn_out, i)
                start = (i // 8) * 128 + half * 64 + i % 8
                for part in range(2):
                    turned[part, pl.ds(start, 8, stride=8), :] = value[part]
    weights = (back[0], back[1])
    for chunk in range(2):
        rows = pl.ds(chunk * 256, 256)
        lines = jnp.concatenate((turned[0, rows, :], turned[1, rows, :]), axis=1)
        result = exact_dot(weights, split(lines), ((1,), (1,)))
        for part in range(2):
            for piece in range(2):
                out[pl.ds(part * 4 + chunk * 2 + piece, 128, stride=8), :] = result[
                    part * 128 : part * 128 + 128, piece * 128 : piece * 128 + 128
                ]


def cells_kernel(arrived, table, matrix, out, left):
    for piece in range(4):
        for part in range(2):
            tile = arrived[pl.ds(part * 4 + piece, 128, stride=8), :]
            left[piece * 128 : piece * 128 + 128, part * 128 : part * 128 + 128] = tile.T
    weights = (matrix[0], matrix[1])
    for chunk in range(2):
        rows = pl.ds(chunk * 256, 256)
        left[rows, :] = exact_dot(split(left[rows, :]), weights, ((1,), (0,)))
    for piece in range(4):
        values = []
        for k in range(16):
            row = piece * 128 + k * 8
            value = (left[row : row + 8, 0:128], left[row : row + 8, 128:256])
            values.append(times(value, table, k))
        modes = [(values[0][0] + values[0][0], None)]
        modes += [add(values[k], conj(values[16 - k])) for k in range(1, 8)]
        modes += [(values[8][0] + values[8][0], None)]
        for c, value in enumerate(real_inverse(modes)):
            out[c, piece * 8 : piece * 8 + 8, :] = value


def call(kernel, out_shape, scratch, flops, **extra):
    return pl.pallas_call(
        kernel,
        out_shape=out_shape,
        scratch_shapes=scratch,
        compiler_params=pltpu.CompilerParams(vmem_limit_bytes=VMEM_LIMIT),
        cost_estimate=pl.CostEstimate(flops=flops, bytes_accessed=4 << 20, transcendentals=0),
        **extra,
    )


def f32(*shape):
    return jax.ShapeDtypeStruct(shape, jnp.float32)


def sum_history(history, windows, first_ky):
    blocks = NX // LANES
    return pl.pallas_call(
        history_kernel,
        grid=(blocks,),
        in_specs=[
            pl.BlockSpec(memory_space=pltpu.SMEM),
            pl.BlockSpec((HIST, 2, 16, LANES), lambda g: (0, 0, 0, g)),
            pl.BlockSpec((16, LANES), lambda g: (0, g)),
        ],
        out_specs=[
            pl.BlockSpec((2, 16, LANES), lambda g: (0, 0, g)),
            pl.BlockSpec((16, LANES), lambda g: (0, g)),
        ],
        out_shape=[f32(2, 16, NX), f32(16, NX)],
        compiler_params=pltpu.CompilerParams(vmem_limit_bytes=VMEM_LIMIT),
        cost_estimate=pl.CostEstimate(
            flops=40_000_000, bytes_accessed=9 << 20, transcendentals=65536
        ),
    )(first_ky, history, windows)


def inverse_sinh(value):
    absolute = jnp.abs(value)
    result = jnp.log(absolute + jnp.sqrt(1.0 + absolute * absolute))
    return jnp.where(value < 0, -result, result)


def on_device(slip, slip_rate, loading, friction, state, history, windows):
    everyone = ("rows", "cols")
    scratch = lambda *shape: pltpu.VMEM(shape, jnp.float32)
    cells = jnp.stack((slip.reshape(16, 32, 128), slip_rate.reshape(16, 32, 128)), 1)
    lines = lax.all_to_all(cells, "cols", split_axis=0, concat_axis=0, tiled=True)

    first_ky = (lax.axis_index(everyone) * 16).astype(jnp.int32).reshape(1)
    summed, waves = sum_history(history, windows, first_ky)

    outbound = call(lines_kernel, f32(2048, 128), [scratch(2, 1024, 128)], 400_000_000)(
        lines, twiddle(16, NY, -1), dft_matrix(-1, 1.0 / math.sqrt(NY), True)
    )
    arrived = lax.all_to_all(
        outbound.reshape(128, 16, 128), everyone, split_axis=0, concat_axis=0, tiled=True
    ).reshape(2048, 128)
    spectrum, outgoing = call(
        modes_kernel,
        [f32(2, 16, NX), f32(1024, 128)],
        [scratch(1024, 256), scratch(1024, 256), scratch(2, 32, 8, 128), scratch(2, 16, NX), scratch(2, 512, 128)],
        600_000_000,
    )(
        arrived,
        summed,
        waves,
        twiddle(32, NX, -1),
        twiddle(32, NX, 1),
        dft_matrix(-1, 1.0 / math.sqrt(NX), False),
        dft_matrix(1, 1.0 / math.sqrt(NX), True),
    )
    returned = lax.all_to_all(
        outgoing.reshape(128, 8, 128), everyone, split_axis=0, concat_axis=0, tiled=True
    ).reshape(1024, 128)
    stress = call(cells_kernel, f32(16, 32, 128), [scratch(512, 256)], 200_000_000)(
        returned, twiddle(16, NY, 1), dft_matrix(1, 0.5 / math.sqrt(NY), False)
    )
    transfer = lax.all_to_all(stress, "cols", split_axis=0, concat_axis=0, tiled=True)
    traction = loading + transfer.reshape(512, 128)
    half_gain = 0.5 * jnp.exp(state)
    velocity = slip_rate
    for sweep in range(NEWTON):
        scaled = velocity * half_gain
        mismatch = friction * inverse_sinh(scaled) + damping * velocity - traction
        tangent = friction * half_gain / jnp.sqrt(1.0 + scaled * scaled) + damping
        velocity = velocity - mismatch / tangent
    return (velocity, traction - damping * velocity, spectrum)


def solution(mesh):
    cell = P("rows", "cols")
    placed = (cell,) * 5 + (P(None, None, ("rows", "cols"), None), P(("rows", "cols"), None))
    return jax.shard_map(
        on_device,
        mesh=mesh,
        in_specs=placed,
        out_specs=(cell, cell, P(None, ("rows", "cols"), None)),
        check_vma=False,
    )
```

```python
import functools
import math

import jax
import jax.numpy as jnp
import ml_dtypes
import numpy as np
from jax import lax
from jax.experimental import pallas as pl
from jax.experimental.pallas import tpu as pltpu
from jax.sharding import PartitionSpec as P

NX = 4096
NY = 2048
HIST = 32
NEWTON = 3
damping = 1.0
LANES = 512
LAGS = 4
VMEM_LIMIT = 24 * 1024 * 1024


def split_host(matrix):
    full = matrix.astype(np.float32)
    high = full.astype(ml_dtypes.bfloat16)
    low = (full - high.astype(np.float32)).astype(ml_dtypes.bfloat16)
    return np.stack((high, low))


def dft_matrix(sign, scale, transposed):
    index = np.arange(128)
    phase = sign * 2.0 * math.pi * (np.outer(index, index) % 128) / 128.0
    cos, sin = np.cos(phase) * scale, np.sin(phase) * scale
    matrix = np.block([[cos, sin], [-sin, cos]])
    return split_host(matrix.T if transposed else matrix)


def twiddle(count, length, sign):
    phase = sign * 2.0 * math.pi * np.outer(np.arange(count), np.arange(128)) / length
    return np.stack((np.cos(phase), np.sin(phase))).astype(np.float32)


def add(a, b):
    return (a[0] + b[0], a[1] + b[1])


def sub(a, b):
    return (a[0] - b[0], a[1] - b[1])


def conj(a):
    return (a[0], -a[1])


def turn(value, numerator, length, sign):
    numerator %= length
    re, im = value
    if numerator == 0:
        return value
    if 4 * numerator == length:
        return (-im, re) if sign > 0 else (im, -re)
    if 2 * numerator == length:
        return (-re, -im)
    if 4 * numerator == 3 * length:
        return (im, -re) if sign > 0 else (-im, re)
    if 8 * numerator % length == 0:
        half = math.sqrt(0.5)
        octant = 8 * numerator // length
        cos_sign = 1.0 if octant in (1, 7) else -1.0
        sin_sign = (1.0 if octant in (1, 3) else -1.0) * sign
        first = re if cos_sign > 0 else -re
        second = im if cos_sign > 0 else -im
        if sin_sign > 0:
            return ((first - im) * half, (re + second) * half)
        return ((first + im) * half, (second - re) * half)
    angle = 2.0 * math.pi * numerator / length
    cos, sin = math.cos(angle), sign * math.sin(angle)
    return (re * cos - im * sin, re * sin + im * cos)


def butterfly(values, sign):
    size = len(values)
    if size == 1:
        return values
    even = butterfly(values[0::2], sign)
    odd = butterfly(values[1::2], sign)
    turned = [turn(odd[k], k, size, sign) for k in range(size // 2)]
    return [add(e, t) for e, t in zip(even, turned)] + [sub(e, t) for e, t in zip(even, turned)]


def real_forward(values):
    size = len(values)
    if size == 2:
        return [(values[0] + values[1], None), (values[0] - values[1], None)]
    even = real_forward(values[0::2])
    odd = real_forward(values[1::2])
    quarter = size // 4
    out = [None] * (size // 2 + 1)
    for k in range(quarter + 1):
        e, o = even[k], odd[k]
        if k == 0:
            out[0] = (e[0] + o[0], None)
            out[size // 2] = (e[0] - o[0], None)
        elif k == quarter:
            out[k] = (e[0], -o[0])
        else:
            t = turn(o, k, size, -1)
            out[k] = add(e, t)
            out[size // 2 - k] = conj(sub(e, t))
    return out


def real_inverse(modes):
    half = len(modes) - 1
    size = 2 * half
    if size == 2:
        return [modes[0][0] + modes[1][0], modes[0][0] - modes[1][0]]
    quarter = half // 2
    even, odd = [], []
    for k in range(quarter + 1):
        a, b = modes[k], modes[half - k]
        if k == 0:
            even.append((a[0] + b[0], None))
            odd.append((a[0] - b[0], None))
        elif k == quarter:
            even.append((a[0] + a[0], None))
            odd.append((-(a[1] + a[1]), None))
        else:
            even.append(add(a, conj(b)))
            odd.append(turn(sub(a, conj(b)), k, size, 1))
    first, second = real_inverse(even), real_inverse(odd)
    out = []
    for e, o in zip(first, second):
        out += [e, o]
    return out


def times(value, table, index, rows=None):
    cos, sin = table[0, index : index + 1, :], table[1, index : index + 1, :]
    re, im = value
    if im is None:
        return (re * cos, re * sin)
    return (re * cos - im * sin, re * sin + im * cos)


def split(value):
    high = value.astype(jnp.bfloat16)
    return high, (value - high.astype(jnp.float32)).astype(jnp.bfloat16)


def dot(left, right, contract):
    return lax.dot_general(
        left, right, ((contract[0], contract[1]), ((), ())), preferred_element_type=jnp.float32
    )


def exact_dot(left, right, contract):
    (lh, ll), (rh, rl) = left, right
    return dot(lh, rh, contract) + (dot(lh, rl, contract) + dot(ll, rh, contract))


def lines_kernel(cells, table, matrix, unused, out, work):
    del unused
    for f in range(2):
        for group in range(4):
            samples = [cells[c, f, 8 * group : 8 * group + 8, :] for c in range(16)]
            modes = real_forward(samples)
            for k in range(16 if f == 1 else 9):
                value = times(modes[k] if k <= 8 else conj(modes[16 - k]), table, k)
                if f == 1:
                    places = [pl.ds(group * 128 + k, 8, stride=16)]
                elif k < 8:
                    places = [pl.ds(512 + group * 64 + k, 8, stride=8)]
                else:
                    places = [pl.ds(768 + 32 * copy + 8 * group, 8) for copy in range(4)]
                for rows in places:
                    work[0, rows, :] = value[0]
                    work[1, rows, :] = value[1]
    weights = (matrix[0], matrix[1])
    for chunk in range(4):
        count = 128 if chunk == 3 else 256
        rows = pl.ds(chunk * 256, count)
        turned = jnp.concatenate((work[0, rows, :], work[1, rows, :]), axis=1)
        result = exact_dot(weights, split(turned), ((1,), (1,)))
        if chunk == 3:
            lane = lax.broadcasted_iota(jnp.int32, (128, 128), 1)
            out[pl.ds(12, 128, stride=13), :] = jnp.where(
                (lane // 32) % 2 == 0, result[0:128], result[128:256]
            )
            continue
        for part in range(2):
            for piece in range(2):
                row = 8 + part * 2 + piece if chunk == 2 else part * 4 + chunk * 2 + piece
                out[pl.ds(row, 128, stride=13), :] = result[
                    part * 128 : part * 128 + 128, piece * 128 : piece * 128 + 128
                ]


def history_kernel(
    first_ky, history, counts, total, waves, stored, windows, cosines, previous, sems
):
    groups = HIST // LAGS
    copies = [pltpu.make_async_copy(counts, windows, sems.at[groups])]
    for group in range(groups):
        lags = pl.ds(group * LAGS, LAGS)
        copies.append(pltpu.make_async_copy(history.at[lags], stored.at[lags], sems.at[group]))
    for copy in copies:
        copy.start()
    copies[0].wait()
    shape = (16, LANES)
    for group in range(groups):
        copies[group + 1].wait()

        @pl.loop(0, NX // LANES)
        def _(block):
            lanes = pl.ds(pl.multiple_of(block * LANES, LANES), LANES)
            if group == 0:
                ky = lax.broadcasted_iota(jnp.int32, shape, 0) + first_ky[0]
                kx = lax.broadcasted_iota(jnp.int32, shape, 1) + block * LANES
                fold_x = jnp.minimum(kx, NX - kx).astype(jnp.float32) * (2.0 / NX)
                fold_y = jnp.minimum(ky, NY - ky).astype(jnp.float32) * (2.0 / NY)
                wave = jnp.sqrt(fold_x * fold_x + fold_y * fold_y)
                waves[:, lanes] = wave
                now = jnp.cos(3.0 * wave)
                double = now + now
                before = jnp.ones(shape, jnp.float32)
                real = jnp.zeros(shape, jnp.float32)
                imag = jnp.zeros(shape, jnp.float32)
                cosines[0, :, lanes] = double
            else:
                double = cosines[0, :, lanes]
                now = cosines[1, :, lanes]
                before = previous[:, lanes]
                real = total[0, :, lanes]
                imag = total[1, :, lanes]
            count = windows[:, lanes]
            for lag in range(group * LAGS + 1, group * LAGS + LAGS + 1):
                if lag > 1:
                    before, now = now, double * now - before
                weight = jnp.where(count >= lag, now * (2.0 * HIST + 2.0 - lag), 0.0)
                real = real + weight * stored[lag - 1, 0, :, lanes].astype(jnp.float32)
                imag = imag + weight * stored[lag - 1, 1, :, lanes].astype(jnp.float32)
            if group == groups - 1:
                factor = (waves[:, lanes] + 0.25) * (-0.5 / (2.0 * HIST + 2.0))
                real = real * factor
                imag = imag * factor
            else:
                cosines[1, :, lanes] = now
                previous[:, lanes] = before
            total[0, :, lanes] = real
            total[1, :, lanes] = imag


def modes_kernel(
    arrived, summed, waves, turn_in, turn_out, into, back, spectrum, out, left, mid, spec, gathered, turned
):
    for part in range(2):
        lanes = slice(part * 128, part * 128 + 128)
        for piece in range(4):
            tile = arrived[pl.ds(part * 4 + piece, 128, stride=13), :]
            left[piece * 128 : piece * 128 + 128, lanes] = tile.T
        for piece in range(2):
            tile = arrived[pl.ds(8 + part * 2 + piece, 128, stride=13), :]
            left[512 + piece * 128 : 640 + piece * 128, lanes] = tile.T
    tile = arrived[pl.ds(12, 128, stride=13), :].T
    left[768:800, 0:128] = tile[0:32]
    left[768:800, 128:256] = tile[32:64]
    weights = (into[0], into[1])
    for piece in range(4):
        rows = pl.ds(piece * 256, 32 if piece == 3 else 256)
        mid[rows, :] = exact_dot(split(left[rows, :]), weights, ((1,), (0,)))
    groups = [(1, 0, 0, 16), (1, 1, 8, 16), (0, 0, 512, 8), (0, 1, 768, 1)]
    for f, half, first, stride in groups:
        for i1 in range(4):
            values = []
            for i2 in range(8):
                i = i1 + 4 * i2
                rows = slice(first + i * stride, first + i * stride + min(stride, 8))
                value = (mid[rows, 0:128], mid[rows, 128:256])
                if stride == 1:
                    value = tuple(jnp.broadcast_to(v, (8, 128)) for v in value)
                values.append(times(value, turn_in, i))
            for b1, value in enumerate(butterfly(values, -1)):
                value = turn(value, i1 * b1, 32, -1)
                spec[0, i1 * 8 + b1] = value[0]
                spec[1, i1 * 8 + b1] = value[1]
        for b1 in range(8):
            values = [(spec[0, i1 * 8 + b1], spec[1, i1 * 8 + b1]) for i1 in range(4)]
            for b2, value in enumerate(butterfly(values, -1)):
                b = b1 + 8 * b2
                for part in range(2):
                    rows = slice(half * 8, half * 8 + 8)
                    lanes = slice(b * 128, b * 128 + 128)
                    if f == 1:
                        spectrum[part, rows, lanes] = value[part]
                    else:
                        gathered[part, rows, lanes] = value[part]
    sublane = lax.broadcasted_iota(jnp.int32, (8, 128), 0)
    for half in range(2):
        rows = slice(half * 8, half * 8 + 8)
        share = jnp.where(sublane == 0, -0.5, -1.0 if half == 0 else 0.0)
        for b1 in range(8):
            values = []
            for b2 in range(4):
                b = b1 + 8 * b2
                lanes = slice(b * 128, b * 128 + 128)
                wave = waves[rows, lanes]
                slip_weight = share * wave
                rate_weight = -0.5 * (wave + 0.25)
                values.append(
                    tuple(
                        slip_weight * gathered[part, rows, lanes]
                        + rate_weight * spectrum[part, rows, lanes]
                        + summed[part, rows, lanes]
                        for part in range(2)
                    )
                )
            for i1, value in enumerate(butterfly(values, 1)):
                value = turn(value, i1 * b1, 32, 1)
                spec[0, i1 * 8 + b1] = value[0]
                spec[1, i1 * 8 + b1] = value[1]
        for i1 in range(4):
            values = [(spec[0, i1 * 8 + b1], spec[1, i1 * 8 + b1]) for b1 in range(8)]
            for i2, value in enumerate(butterfly(values, 1)):
                i = i1 + 4 * i2
                value = times(value, turn_out, i)
                start = (i // 8) * 128 + half * 64 + i % 8
                for part in range(2):
                    turned[part, pl.ds(start, 8, stride=8), :] = value[part]
    weights = (back[0], back[1])
    for chunk in range(2):
        rows = pl.ds(chunk * 256, 256)
        lines = jnp.concatenate((turned[0, rows, :], turned[1, rows, :]), axis=1)
        result = exact_dot(weights, split(lines), ((1,), (1,)))
        for part in range(2):
            for piece in range(2):
                out[pl.ds(part * 4 + chunk * 2 + piece, 128, stride=8), :] = result[
                    part * 128 : part * 128 + 128, piece * 128 : piece * 128 + 128
                ]


def cells_kernel(arrived, table, matrix, out, left):
    for piece in range(4):
        for part in range(2):
            tile = arrived[pl.ds(part * 4 + piece, 128, stride=8), :]
            left[piece * 128 : piece * 128 + 128, part * 128 : part * 128 + 128] = tile.T
    weights = (matrix[0], matrix[1])
    for chunk in range(2):
        rows = pl.ds(chunk * 256, 256)
        left[rows, :] = exact_dot(split(left[rows, :]), weights, ((1,), (0,)))
    for piece in range(4):
        values = []
        for k in range(16):
            row = piece * 128 + k * 8
            value = (left[row : row + 8, 0:128], left[row : row + 8, 128:256])
            values.append(times(value, table, k))
        modes = [(values[0][0] + values[0][0], None)]
        modes += [add(values[k], conj(values[16 - k])) for k in range(1, 8)]
        modes += [(values[8][0] + values[8][0], None)]
        for c, value in enumerate(real_inverse(modes)):
            out[c, piece * 8 : piece * 8 + 8, :] = value


def call(kernel, out_shape, scratch, flops, **extra):
    return pl.pallas_call(
        kernel,
        out_shape=out_shape,
        scratch_shapes=scratch,
        compiler_params=pltpu.CompilerParams(vmem_limit_bytes=VMEM_LIMIT),
        cost_estimate=pl.CostEstimate(flops=flops, bytes_accessed=4 << 20, transcendentals=0),
        **extra,
    )


def f32(*shape):
    return jax.ShapeDtypeStruct(shape, jnp.float32)


def sum_history(history, windows, first_ky):
    remote = pl.BlockSpec(memory_space=pl.ANY)
    return pl.pallas_call(
        history_kernel,
        in_specs=[pl.BlockSpec(memory_space=pltpu.SMEM), remote, remote],
        out_shape=[f32(2, 16, NX), f32(16, NX)],
        scratch_shapes=[
            pltpu.VMEM((HIST, 2, 16, NX), jnp.bfloat16),
            pltpu.VMEM((16, NX), jnp.int32),
            pltpu.VMEM((2, 16, NX), jnp.float32),
            pltpu.VMEM((16, NX), jnp.float32),
            pltpu.SemaphoreType.DMA((HIST // LAGS + 1,)),
        ],
        compiler_params=pltpu.CompilerParams(vmem_limit_bytes=VMEM_LIMIT),
        cost_estimate=pl.CostEstimate(
            flops=40_000_000, bytes_accessed=9 << 20, transcendentals=65536
        ),
    )(
        first_ky,
        pltpu.with_memory_space_constraint(history, pltpu.HBM),
        pltpu.with_memory_space_constraint(windows, pltpu.HBM),
    )


def on_device(slip, slip_rate, loading, friction, state, history, windows):
    everyone = ("rows", "cols")
    scratch = lambda *shape: pltpu.VMEM(shape, jnp.float32)
    whole = pl.BlockSpec(memory_space=pltpu.VMEM)
    remote = pl.BlockSpec(memory_space=pl.ANY)
    cells = jnp.stack((slip.reshape(16, 32, 128), slip_rate.reshape(16, 32, 128)), 1)
    lines = lax.all_to_all(cells, "cols", split_axis=0, concat_axis=0, tiled=True)

    first_ky = (lax.axis_index(everyone) * 16).astype(jnp.int32).reshape(1)
    summed, waves = sum_history(history, windows, first_ky)

    outbound = call(
        lines_kernel,
        f32(1664, 128),
        [scratch(2, 896, 128)],
        400_000_000,
        in_specs=[whole] * 3 + [remote],
    )(lines, twiddle(16, NY, -1), dft_matrix(-1, 1.0 / math.sqrt(NY), True), waves)
    arrived = lax.all_to_all(
        outbound.reshape(128, 13 * 128), everyone, split_axis=0, concat_axis=0, tiled=True
    ).reshape(1664, 128)
    spectrum, outgoing = call(
        modes_kernel,
        [f32(2, 16, NX), f32(1024, 128)],
        [
            scratch(800, 256),
            scratch(800, 256),
            scratch(2, 32, 8, 128),
            scratch(2, 16, NX),
            scratch(2, 512, 128),
        ],
        600_000_000,
    )(
        arrived,
        summed,
        waves,
        twiddle(32, NX, -1),
        twiddle(32, NX, 1),
        dft_matrix(-1, 1.0 / math.sqrt(NX), False),
        dft_matrix(1, 1.0 / math.sqrt(NX), True),
    )
    returned = lax.all_to_all(
        outgoing.reshape(128, 8, 128), everyone, split_axis=0, concat_axis=0, tiled=True
    ).reshape(1024, 128)
    stress = call(cells_kernel, f32(16, 32, 128), [scratch(512, 256)], 200_000_000)(
        returned, twiddle(16, NY, 1), dft_matrix(1, 0.5 / math.sqrt(NY), False)
    )
    transfer = lax.all_to_all(stress, "cols", split_axis=0, concat_axis=0, tiled=True)
    transfer = transfer.reshape(512, 128)

    traction = loading + transfer
    half_gain = 0.5 * jnp.exp(state)
    steepness = friction * half_gain
    velocity = slip_rate
    for sweep in range(NEWTON):
        scaled = velocity * half_gain
        root = jnp.sqrt(1.0 + scaled * scaled)
        magnitude = jnp.log(jnp.abs(scaled) + root)
        mismatch = friction * jnp.where(scaled < 0, -magnitude, magnitude) + damping * velocity - traction
        velocity = velocity - mismatch * root / (steepness + damping * root)
    return (velocity, traction - damping * velocity, spectrum)


def solution(mesh):
    cell = P("rows", "cols")
    placed = (cell,) * 5 + (P(None, None, ("rows", "cols"), None), P(("rows", "cols"), None))
    return jax.shard_map(
        on_device,
        mesh=mesh,
        in_specs=placed,
        out_specs=(cell, cell, P(None, ("rows", "cols"), None)),
        check_vma=False,
    )
```

```python
import functools
import math

import jax
import jax.numpy as jnp
import ml_dtypes
import numpy as np
from jax import lax
from jax.experimental import pallas as pl
from jax.experimental.pallas import tpu as pltpu
from jax.sharding import PartitionSpec as P

NX = 4096
NY = 2048
HIST = 32
NEWTON = 3
damping = 1.0
LANES = 512
LAGS = 4
VMEM_LIMIT = 24 * 1024 * 1024


def split_host(matrix):
    full = matrix.astype(np.float32)
    high = full.astype(ml_dtypes.bfloat16)
    low = (full - high.astype(np.float32)).astype(ml_dtypes.bfloat16)
    return np.stack((high, low))


def dft_matrix(sign, scale, transposed):
    index = np.arange(128)
    phase = sign * 2.0 * math.pi * (np.outer(index, index) % 128) / 128.0
    cos, sin = np.cos(phase) * scale, np.sin(phase) * scale
    matrix = np.block([[cos, sin], [-sin, cos]])
    return split_host(matrix.T if transposed else matrix)


def twiddle(count, length, sign):
    phase = sign * 2.0 * math.pi * np.outer(np.arange(count), np.arange(128)) / length
    return np.stack((np.cos(phase), np.sin(phase))).astype(np.float32)


def nyquist_waves():
    kx = np.arange(NX, dtype=np.float32)
    fold = np.minimum(kx, NX - kx) * np.float32(2.0 / NX)
    return np.sqrt(fold * fold + np.float32(1.0)).reshape(32, 128)


def add(a, b):
    return (a[0] + b[0], a[1] + b[1])


def sub(a, b):
    return (a[0] - b[0], a[1] - b[1])


def conj(a):
    return (a[0], -a[1])


def turn(value, numerator, length, sign):
    numerator %= length
    re, im = value
    if numerator == 0:
        return value
    if 4 * numerator == length:
        return (-im, re) if sign > 0 else (im, -re)
    if 2 * numerator == length:
        return (-re, -im)
    if 4 * numerator == 3 * length:
        return (im, -re) if sign > 0 else (-im, re)
    if 8 * numerator % length == 0:
        half = math.sqrt(0.5)
        octant = 8 * numerator // length
        cos_sign = 1.0 if octant in (1, 7) else -1.0
        sin_sign = (1.0 if octant in (1, 3) else -1.0) * sign
        first = re if cos_sign > 0 else -re
        second = im if cos_sign > 0 else -im
        if sin_sign > 0:
            return ((first - im) * half, (re + second) * half)
        return ((first + im) * half, (second - re) * half)
    angle = 2.0 * math.pi * numerator / length
    cos, sin = math.cos(angle), sign * math.sin(angle)
    return (re * cos - im * sin, re * sin + im * cos)


def butterfly(values, sign):
    size = len(values)
    if size == 1:
        return values
    even = butterfly(values[0::2], sign)
    odd = butterfly(values[1::2], sign)
    turned = [turn(odd[k], k, size, sign) for k in range(size // 2)]
    return [add(e, t) for e, t in zip(even, turned)] + [sub(e, t) for e, t in zip(even, turned)]


def real_forward(values):
    size = len(values)
    if size == 2:
        return [(values[0] + values[1], None), (values[0] - values[1], None)]
    even = real_forward(values[0::2])
    odd = real_forward(values[1::2])
    quarter = size // 4
    out = [None] * (size // 2 + 1)
    for k in range(quarter + 1):
        e, o = even[k], odd[k]
        if k == 0:
            out[0] = (e[0] + o[0], None)
            out[size // 2] = (e[0] - o[0], None)
        elif k == quarter:
            out[k] = (e[0], -o[0])
        else:
            t = turn(o, k, size, -1)
            out[k] = add(e, t)
            out[size // 2 - k] = conj(sub(e, t))
    return out


def real_inverse(modes):
    half = len(modes) - 1
    size = 2 * half
    if size == 2:
        return [modes[0][0] + modes[1][0], modes[0][0] - modes[1][0]]
    quarter = half // 2
    even, odd = [], []
    for k in range(quarter + 1):
        a, b = modes[k], modes[half - k]
        if k == 0:
            even.append((a[0] + b[0], None))
            odd.append((a[0] - b[0], None))
        elif k == quarter:
            even.append((a[0] + a[0], None))
            odd.append((-(a[1] + a[1]), None))
        else:
            even.append(add(a, conj(b)))
            odd.append(turn(sub(a, conj(b)), k, size, 1))
    first, second = real_inverse(even), real_inverse(odd)
    out = []
    for e, o in zip(first, second):
        out += [e, o]
    return out


def times(value, table, index, rows=None):
    cos, sin = table[0, index : index + 1, :], table[1, index : index + 1, :]
    re, im = value
    if im is None:
        return (re * cos, re * sin)
    return (re * cos - im * sin, re * sin + im * cos)


def split(value):
    high = value.astype(jnp.bfloat16)
    return high, (value - high.astype(jnp.float32)).astype(jnp.bfloat16)


def dot(left, right, contract):
    return lax.dot_general(
        left, right, ((contract[0], contract[1]), ((), ())), preferred_element_type=jnp.float32
    )


def exact_dot(left, right, contract):
    (lh, ll), (rh, rl) = left, right
    return dot(lh, rh, contract) + (dot(lh, rl, contract) + dot(ll, rh, contract))


def lines_kernel(cells, table, matrix, unused, out, work):
    del unused
    for f in range(2):
        for group in range(4):
            samples = [cells[c, f, 8 * group : 8 * group + 8, :] for c in range(16)]
            modes = real_forward(samples)
            for k in range(16 if f == 1 else 9):
                value = times(modes[k] if k <= 8 else conj(modes[16 - k]), table, k)
                if f == 1:
                    places = [pl.ds(group * 128 + k, 8, stride=16)]
                elif k < 8:
                    places = [pl.ds(512 + group * 64 + k, 8, stride=8)]
                else:
                    places = [pl.ds(768 + group * 64 + slot, 8, stride=8) for slot in range(8)]
                for rows in places:
                    work[0, rows, :] = value[0]
                    work[1, rows, :] = value[1]
    weights = (matrix[0], matrix[1])

    def transform(chunk):
        rows = pl.ds(chunk * 256, 256)
        turned = jnp.concatenate((work[0, rows, :], work[1, rows, :]), axis=1)
        return exact_dot(weights, split(turned), ((1,), (1,)))

    def tile_of(result, part, piece):
        return result[part * 128 : part * 128 + 128, piece * 128 : piece * 128 + 128]

    for chunk in range(2):
        result = transform(chunk)
        for part in range(2):
            for piece in range(2):
                out[pl.ds(part * 4 + chunk * 2 + piece, 128, stride=12), :] = tile_of(
                    result, part, piece
                )
    lower, upper = transform(2), transform(3)
    owner = lax.broadcasted_iota(jnp.int32, (128, 128), 0)
    first_slot = lax.broadcasted_iota(jnp.int32, (128, 128), 1) % 8 == 0
    for part in range(2):
        for piece in range(2):
            tile = jnp.where(
                first_slot & (owner >= 64), tile_of(upper, part, piece), tile_of(lower, part, piece)
            )
            if part == 1:
                nyquist = lower[64:65, piece * 128 : piece * 128 + 128]
                tile = jnp.where(first_slot & (owner == 0), nyquist, tile)
            out[pl.ds(8 + part * 2 + piece, 128, stride=12), :] = tile


def history_kernel(
    first_ky, history, counts, total, waves, stored, windows, cosines, previous, sems
):
    groups = HIST // LAGS
    copies = [pltpu.make_async_copy(counts, windows, sems.at[groups])]
    for group in range(groups):
        lags = pl.ds(group * LAGS, LAGS)
        copies.append(pltpu.make_async_copy(history.at[lags], stored.at[lags], sems.at[group]))
    for copy in copies:
        copy.start()
    shape = (16, LANES)

    @pl.loop(0, NX // LANES)
    def _(block):
        lanes = pl.ds(pl.multiple_of(block * LANES, LANES), LANES)
        ky = lax.broadcasted_iota(jnp.int32, shape, 0) + first_ky[0]
        kx = lax.broadcasted_iota(jnp.int32, shape, 1) + block * LANES
        fold_x = jnp.minimum(kx, NX - kx).astype(jnp.float32) * (2.0 / NX)
        fold_y = jnp.minimum(ky, NY - ky).astype(jnp.float32) * (2.0 / NY)
        wave = jnp.sqrt(fold_x * fold_x + fold_y * fold_y)
        waves[:, lanes] = wave
        cosines[1, :, lanes] = jnp.cos(3.0 * wave)

    copies[0].wait()
    for group in range(groups):
        copies[group + 1].wait()

        @pl.loop(0, NX // LANES)
        def _(block):
            lanes = pl.ds(pl.multiple_of(block * LANES, LANES), LANES)
            now = cosines[1, :, lanes]
            double = now + now
            if group == 0:
                cosines[0, :, lanes] = double
                before = jnp.ones(shape, jnp.float32)
                real = jnp.zeros(shape, jnp.float32)
                imag = jnp.zeros(shape, jnp.float32)
            else:
                double = cosines[0, :, lanes]
                before = previous[:, lanes]
                real = total[0, :, lanes]
                imag = total[1, :, lanes]
            count = windows[:, lanes]
            for lag in range(group * LAGS + 1, group * LAGS + LAGS + 1):
                if lag > 1:
                    before, now = now, double * now - before
                weight = jnp.where(count >= lag, now * (2.0 * HIST + 2.0 - lag), 0.0)
                real = real + weight * stored[lag - 1, 0, :, lanes].astype(jnp.float32)
                imag = imag + weight * stored[lag - 1, 1, :, lanes].astype(jnp.float32)
            if group == groups - 1:
                factor = (waves[:, lanes] + 0.25) * (-0.5 / (2.0 * HIST + 2.0))
                real = real * factor
                imag = imag * factor
            else:
                cosines[1, :, lanes] = now
                previous[:, lanes] = before
            total[0, :, lanes] = real
            total[1, :, lanes] = imag


def modes_kernel(
    first_ky,
    arrived,
    summed,
    waves,
    turn_in,
    turn_out,
    into,
    back,
    nyquist_wave,
    spectrum_out,
    out,
    left,
    mid,
    spec,
    gathered,
    spectrum,
    turned,
    sem,
):
    for part in range(2):
        lanes = slice(part * 128, part * 128 + 128)
        for piece in range(4):
            tile = arrived[pl.ds(part * 4 + piece, 128, stride=12), :]
            left[piece * 128 : piece * 128 + 128, lanes] = tile.T
        for piece in range(2):
            tile = arrived[pl.ds(8 + part * 2 + piece, 128, stride=12), :]
            left[512 + piece * 128 : 640 + piece * 128, lanes] = tile.T
    weights = (into[0], into[1])
    for piece in range(3):
        rows = pl.ds(piece * 256, 256)
        mid[rows, :] = exact_dot(split(left[rows, :]), weights, ((1,), (0,)))
    for f, half, first, stride in [(1, 0, 0, 16), (1, 1, 8, 16), (0, 0, 512, 8)]:
        for i1 in range(4):
            values = []
            for i2 in range(8):
                i = i1 + 4 * i2
                rows = slice(first + i * stride, first + i * stride + 8)
                values.append(times((mid[rows, 0:128], mid[rows, 128:256]), turn_in, i))
            for b1, value in enumerate(butterfly(values, -1)):
                value = turn(value, i1 * b1, 32, -1)
                spec[0, i1 * 8 + b1] = value[0]
                spec[1, i1 * 8 + b1] = value[1]
        for b1 in range(8):
            values = [(spec[0, i1 * 8 + b1], spec[1, i1 * 8 + b1]) for i1 in range(4)]
            for b2, value in enumerate(butterfly(values, -1)):
                b = b1 + 8 * b2
                for part in range(2):
                    rows = slice(half * 8, half * 8 + 8)
                    lanes = slice(b * 128, b * 128 + 128)
                    if f == 1:
                        spectrum[part, rows, lanes] = value[part]
                    else:
                        gathered[part, :, lanes] = value[part]
        if f == 1 and half == 1:
            finished = pltpu.make_async_copy(spectrum, spectrum_out, sem)
            finished.start()
    sublane = lax.broadcasted_iota(jnp.int32, (8, 128), 0)
    first = first_ky[0]
    share_zero = jnp.where(first == 0, -0.5, jnp.where(first < NY // 2, -1.0, 0.0))
    share_eight = jnp.where(first < NY // 2, 0.0, -1.0)
    shares = (jnp.where(sublane == 0, share_zero, -1.0), jnp.where(sublane == 0, share_eight, 0.0))
    for half in range(3):
        rows = slice(half * 8, half * 8 + 8)
        for b1 in range(8):
            values = []
            for b2 in range(4):
                b = b1 + 8 * b2
                lanes = slice(b * 128, b * 128 + 128)
                if half == 2:
                    weight = nyquist_wave[b : b + 1, :] * -0.5
                    values.append(
                        tuple(
                            jnp.broadcast_to(gathered[part, 0:1, lanes] * weight, (8, 128))
                            for part in range(2)
                        )
                    )
                    continue
                wave = waves[rows, lanes]
                slip_weight = shares[half] * wave
                rate_weight = -0.5 * (wave + 0.25)
                values.append(
                    tuple(
                        slip_weight * gathered[part, :, lanes]
                        + rate_weight * spectrum[part, rows, lanes]
                        + summed[part, rows, lanes]
                        for part in range(2)
                    )
                )
            for i1, value in enumerate(butterfly(values, 1)):
                value = turn(value, i1 * b1, 32, 1)
                spec[0, i1 * 8 + b1] = value[0]
                spec[1, i1 * 8 + b1] = value[1]
        for i1 in range(4):
            values = [(spec[0, i1 * 8 + b1], spec[1, i1 * 8 + b1]) for b1 in range(8)]
            for i2, value in enumerate(butterfly(values, 1)):
                i = i1 + 4 * i2
                value = times(value, turn_out, i)
                start = (i // 8) * 128 + half * 64 + i % 8
                for part in range(2):
                    if half == 2:
                        turned[part, 512 + i : 513 + i, :] = value[part][0:1, :]
                    else:
                        turned[part, pl.ds(start, 8, stride=8), :] = value[part]
    weights = (back[0], back[1])

    def transform(rows, weights):
        lines = jnp.concatenate((turned[0, rows, :], turned[1, rows, :]), axis=1)
        return exact_dot(weights, split(lines), ((1,), (1,)))

    nyquist = transform(pl.ds(512, 128), (back[0, 128:256], back[1, 128:256]))
    lane = lax.broadcasted_iota(jnp.int32, (128, 128), 1)
    for chunk in range(2):
        result = transform(pl.ds(chunk * 256, 256), weights)
        for part in range(2):
            for piece in range(2):
                tile = result[part * 128 : part * 128 + 128, piece * 128 : piece * 128 + 128]
                group = chunk * 2 + piece
                if part == 1:
                    moved = pltpu.roll(nyquist, (128 - 8 * group) % 128, 1)
                    tile = jnp.where((lane < 8) & (first == 0), moved, tile)
                out[pl.ds(part * 4 + group, 128, stride=8), :] = tile
    finished.wait()


def cells_kernel(arrived, table, matrix, out, left):
    for piece in range(4):
        for part in range(2):
            tile = arrived[pl.ds(part * 4 + piece, 128, stride=8), :]
            left[piece * 128 : piece * 128 + 128, part * 128 : part * 128 + 128] = tile.T
    edges = [left[piece * 128 : piece * 128 + 8, 128:129] for piece in range(4)]
    parity = lax.broadcasted_iota(jnp.int32, (8, 128), 1) % 2
    alternating = jnp.where(parity == 0, 1.0, -1.0) * (0.5 / math.sqrt(NY))
    weights = (matrix[0], matrix[1])
    for chunk in range(2):
        rows = pl.ds(chunk * 256, 256)
        left[rows, :] = exact_dot(split(left[rows, :]), weights, ((1,), (0,)))
    for piece in range(4):
        values = []
        for k in range(16):
            row = piece * 128 + k * 8
            value = (left[row : row + 8, 0:128], left[row : row + 8, 128:256])
            values.append(times(value, table, k))
        constant = values[0][0] + alternating * edges[piece]
        modes = [(constant + constant, None)]
        modes += [add(values[k], conj(values[16 - k])) for k in range(1, 8)]
        modes += [(values[8][0] + values[8][0], None)]
        for c, value in enumerate(real_inverse(modes)):
            out[c, piece * 8 : piece * 8 + 8, :] = value


def call(kernel, out_shape, scratch, flops, **extra):
    return pl.pallas_call(
        kernel,
        out_shape=out_shape,
        scratch_shapes=scratch,
        compiler_params=pltpu.CompilerParams(vmem_limit_bytes=VMEM_LIMIT),
        cost_estimate=pl.CostEstimate(flops=flops, bytes_accessed=4 << 20, transcendentals=0),
        **extra,
    )


def f32(*shape):
    return jax.ShapeDtypeStruct(shape, jnp.float32)


def sum_history(history, windows, first_ky):
    remote = pl.BlockSpec(memory_space=pl.ANY)
    return pl.pallas_call(
        history_kernel,
        in_specs=[pl.BlockSpec(memory_space=pltpu.SMEM), remote, remote],
        out_shape=[f32(2, 16, NX), f32(16, NX)],
        scratch_shapes=[
            pltpu.VMEM((HIST, 2, 16, NX), jnp.bfloat16),
            pltpu.VMEM((16, NX), jnp.int32),
            pltpu.VMEM((2, 16, NX), jnp.float32),
            pltpu.VMEM((16, NX), jnp.float32),
            pltpu.SemaphoreType.DMA((HIST // LAGS + 1,)),
        ],
        compiler_params=pltpu.CompilerParams(vmem_limit_bytes=VMEM_LIMIT),
        cost_estimate=pl.CostEstimate(
            flops=40_000_000, bytes_accessed=9 << 20, transcendentals=65536
        ),
    )(
        first_ky,
        pltpu.with_memory_space_constraint(history, pltpu.HBM),
        pltpu.with_memory_space_constraint(windows, pltpu.HBM),
    )


def on_device(slip, slip_rate, loading, friction, state, history, windows):
    everyone = ("rows", "cols")
    scratch = lambda *shape: pltpu.VMEM(shape, jnp.float32)
    whole = pl.BlockSpec(memory_space=pltpu.VMEM)
    remote = pl.BlockSpec(memory_space=pl.ANY)
    cells = jnp.stack((slip.reshape(16, 32, 128), slip_rate.reshape(16, 32, 128)), 1)
    lines = lax.all_to_all(cells, "cols", split_axis=0, concat_axis=0, tiled=True)

    first_ky = (lax.axis_index(everyone) * 16).astype(jnp.int32).reshape(1)
    summed, waves = sum_history(history, windows, first_ky)

    outbound = call(
        lines_kernel,
        f32(1536, 128),
        [scratch(2, 1024, 128)],
        400_000_000,
        in_specs=[whole] * 3 + [remote],
    )(lines, twiddle(16, NY, -1), dft_matrix(-1, 1.0 / math.sqrt(NY), True), waves)
    arrived = lax.all_to_all(
        outbound.reshape(128, 12 * 128), everyone, split_axis=0, concat_axis=0, tiled=True
    ).reshape(1536, 128)
    spectrum, outgoing = call(
        modes_kernel,
        [f32(2, 16, NX), f32(1024, 128)],
        [
            scratch(768, 256),
            scratch(768, 256),
            scratch(2, 32, 8, 128),
            scratch(2, 8, NX),
            scratch(2, 16, NX),
            scratch(2, 640, 128),
            pltpu.SemaphoreType.DMA,
        ],
        600_000_000,
        in_specs=[pl.BlockSpec(memory_space=pltpu.SMEM)] + [whole] * 8,
        out_specs=[remote, whole],
    )(
        first_ky,
        arrived,
        summed,
        waves,
        twiddle(32, NX, -1),
        twiddle(32, NX, 1),
        dft_matrix(-1, 1.0 / math.sqrt(NX), False),
        dft_matrix(1, 1.0 / math.sqrt(NX), True),
        nyquist_waves(),
    )
    returned = lax.all_to_all(
        outgoing.reshape(128, 8, 128), everyone, split_axis=0, concat_axis=0, tiled=True
    ).reshape(1024, 128)
    stress = call(cells_kernel, f32(16, 32, 128), [scratch(512, 256)], 200_000_000)(
        returned, twiddle(16, NY, 1), dft_matrix(1, 0.5 / math.sqrt(NY), False)
    )
    transfer = lax.all_to_all(stress, "cols", split_axis=0, concat_axis=0, tiled=True)
    transfer = transfer.reshape(512, 128)

    traction = loading + transfer
    half_gain = 0.5 * jnp.exp(state)
    steepness = friction * half_gain
    velocity = slip_rate
    for sweep in range(NEWTON):
        scaled = velocity * half_gain
        square = 1.0 + scaled * scaled
        root = square * lax.rsqrt(square)
        magnitude = jnp.log(jnp.abs(scaled) + root)
        mismatch = friction * jnp.where(scaled < 0, -magnitude, magnitude) + damping * velocity - traction
        velocity = velocity - mismatch * root / (steepness + damping * root)
    return (velocity, traction - damping * velocity, spectrum)


def solution(mesh):
    cell = P("rows", "cols")
    placed = (cell,) * 5 + (P(None, None, ("rows", "cols"), None), P(("rows", "cols"), None))
    return jax.shard_map(
        on_device,
        mesh=mesh,
        in_specs=placed,
        out_specs=(cell, cell, P(None, ("rows", "cols"), None)),
        check_vma=False,
    )
```

```python
import functools
import math

import jax
import jax.numpy as jnp
import ml_dtypes
import numpy as np
from jax import lax
from jax.experimental import pallas as pl
from jax.experimental.pallas import tpu as pltpu
from jax.sharding import PartitionSpec as P

NX = 4096
NY = 2048
HIST = 32
NEWTON = 3
damping = 1.0
LANES = 512
LAGS = 4
VMEM_LIMIT = 24 * 1024 * 1024


def split_host(matrix):
    full = matrix.astype(np.float32)
    high = full.astype(ml_dtypes.bfloat16)
    low = (full - high.astype(np.float32)).astype(ml_dtypes.bfloat16)
    return np.stack((high, low))


def dft_matrix(sign, scale, transposed):
    index = np.arange(128)
    phase = sign * 2.0 * math.pi * (np.outer(index, index) % 128) / 128.0
    cos, sin = np.cos(phase) * scale, np.sin(phase) * scale
    matrix = np.block([[cos, sin], [-sin, cos]])
    return split_host(matrix.T if transposed else matrix)


def twiddle(count, length, sign):
    phase = sign * 2.0 * math.pi * np.outer(np.arange(count), np.arange(128)) / length
    return np.stack((np.cos(phase), np.sin(phase))).astype(np.float32)


def nyquist_waves():
    kx = np.arange(NX, dtype=np.float32)
    fold = np.minimum(kx, NX - kx) * np.float32(2.0 / NX)
    return np.sqrt(fold * fold + np.float32(1.0)).reshape(32, 128)


def add(a, b):
    return (a[0] + b[0], a[1] + b[1])


def sub(a, b):
    return (a[0] - b[0], a[1] - b[1])


def conj(a):
    return (a[0], -a[1])


def turn(value, numerator, length, sign):
    numerator %= length
    re, im = value
    if numerator == 0:
        return value
    if 4 * numerator == length:
        return (-im, re) if sign > 0 else (im, -re)
    if 2 * numerator == length:
        return (-re, -im)
    if 4 * numerator == 3 * length:
        return (im, -re) if sign > 0 else (-im, re)
    if 8 * numerator % length == 0:
        half = math.sqrt(0.5)
        octant = 8 * numerator // length
        cos_sign = 1.0 if octant in (1, 7) else -1.0
        sin_sign = (1.0 if octant in (1, 3) else -1.0) * sign
        first = re if cos_sign > 0 else -re
        second = im if cos_sign > 0 else -im
        if sin_sign > 0:
            return ((first - im) * half, (re + second) * half)
        return ((first + im) * half, (second - re) * half)
    angle = 2.0 * math.pi * numerator / length
    cos, sin = math.cos(angle), sign * math.sin(angle)
    return (re * cos - im * sin, re * sin + im * cos)


def butterfly(values, sign):
    size = len(values)
    if size == 1:
        return values
    even = butterfly(values[0::2], sign)
    odd = butterfly(values[1::2], sign)
    turned = [turn(odd[k], k, size, sign) for k in range(size // 2)]
    return [add(e, t) for e, t in zip(even, turned)] + [sub(e, t) for e, t in zip(even, turned)]


def real_forward(values):
    size = len(values)
    if size == 2:
        return [(values[0] + values[1], None), (values[0] - values[1], None)]
    even = real_forward(values[0::2])
    odd = real_forward(values[1::2])
    quarter = size // 4
    out = [None] * (size // 2 + 1)
    for k in range(quarter + 1):
        e, o = even[k], odd[k]
        if k == 0:
            out[0] = (e[0] + o[0], None)
            out[size // 2] = (e[0] - o[0], None)
        elif k == quarter:
            out[k] = (e[0], -o[0])
        else:
            t = turn(o, k, size, -1)
            out[k] = add(e, t)
            out[size // 2 - k] = conj(sub(e, t))
    return out


def real_inverse(modes):
    half = len(modes) - 1
    size = 2 * half
    if size == 2:
        return [modes[0][0] + modes[1][0], modes[0][0] - modes[1][0]]
    quarter = half // 2
    even, odd = [], []
    for k in range(quarter + 1):
        a, b = modes[k], modes[half - k]
        if k == 0:
            even.append((a[0] + b[0], None))
            odd.append((a[0] - b[0], None))
        elif k == quarter:
            even.append((a[0] + a[0], None))
            odd.append((-(a[1] + a[1]), None))
        else:
            even.append(add(a, conj(b)))
            odd.append(turn(sub(a, conj(b)), k, size, 1))
    first, second = real_inverse(even), real_inverse(odd)
    out = []
    for e, o in zip(first, second):
        out += [e, o]
    return out


def times(value, table, index, rows=None):
    cos, sin = table[0, index : index + 1, :], table[1, index : index + 1, :]
    re, im = value
    if im is None:
        return (re * cos, re * sin)
    return (re * cos - im * sin, re * sin + im * cos)


def first_wavenumber():
    return lax.axis_index(("rows", "cols")) * 16


def split(value):
    high = value.astype(jnp.bfloat16)
    return high, (value - high.astype(jnp.float32)).astype(jnp.bfloat16)


def dot(left, right):
    return jnp.dot(left, right, preferred_element_type=jnp.float32)


def dot_transposed(left, right):
    return lax.dot_general(
        left, right, (((1,), (1,)), ((), ())), preferred_element_type=jnp.float32
    )


def exact_dot(data, matrix):
    (high, low), (matrix_high, matrix_low) = data, matrix
    count = matrix_high.shape[1]
    wide = dot(high, jnp.concatenate((matrix_high, matrix_low), axis=1))
    return wide[:, :count] + (wide[:, count:] + dot(low, matrix_high))


def lines_kernel(cells, table, matrix, unused, out, work):
    del unused
    for f in range(2):
        for group in range(4):
            samples = [cells[c, f, 8 * group : 8 * group + 8, :] for c in range(16)]
            modes = real_forward(samples)
            for k in range(16 if f == 1 else 9):
                value = times(modes[k] if k <= 8 else conj(modes[16 - k]), table, k)
                if f == 1:
                    places = [pl.ds(group * 128 + k, 8, stride=16)]
                elif k < 8:
                    places = [pl.ds(512 + group * 64 + k, 8, stride=8)]
                else:
                    places = [pl.ds(768 + group * 64 + slot, 8, stride=8) for slot in range(8)]
                for rows in places:
                    work[0, rows, :] = value[0]
                    work[1, rows, :] = value[1]
    weights = (matrix[0], matrix[1])

    def transform(chunk):
        rows = pl.ds(chunk * 256, 256)
        turned = jnp.concatenate((work[0, rows, :], work[1, rows, :]), axis=1)
        high, low = split(turned)
        return dot_transposed(weights[0], high) + (
            dot_transposed(weights[1], high) + dot_transposed(weights[0], low)
        )

    def tile_of(result, part, piece):
        return result[part * 128 : part * 128 + 128, piece * 128 : piece * 128 + 128]

    for chunk in range(2):
        result = transform(chunk)
        for part in range(2):
            for piece in range(2):
                out[pl.ds(part * 4 + chunk * 2 + piece, 128, stride=12), :] = tile_of(
                    result, part, piece
                )
    lower, upper = transform(2), transform(3)
    owner = lax.broadcasted_iota(jnp.int32, (128, 128), 0)
    first_slot = lax.broadcasted_iota(jnp.int32, (128, 128), 1) % 8 == 0
    for part in range(2):
        for piece in range(2):
            tile = jnp.where(
                first_slot & (owner >= 64), tile_of(upper, part, piece), tile_of(lower, part, piece)
            )
            if part == 1:
                nyquist = lower[64:65, piece * 128 : piece * 128 + 128]
                tile = jnp.where(first_slot & (owner == 0), nyquist, tile)
            out[pl.ds(8 + part * 2 + piece, 128, stride=12), :] = tile


def early_kernel(
    history, counts, rate, loading, friction, state, total, waves, start, inverse, stored, windows, cells, cosines, previous, sems
):
    groups = HIST // LAGS
    copies = [pltpu.make_async_copy(counts, windows, sems.at[groups])]
    for group in range(groups):
        lags = pl.ds(group * LAGS, LAGS)
        copies.append(pltpu.make_async_copy(history.at[lags], stored.at[lags], sems.at[group]))
    for index, field in enumerate((rate, loading, friction, state)):
        copies.append(pltpu.make_async_copy(field, cells.at[index], sems.at[groups + 1 + index]))
    for copy in copies:
        copy.start()
    shape = (16, LANES)

    @pl.loop(0, NX // LANES)
    def _(block):
        lanes = pl.ds(pl.multiple_of(block * LANES, LANES), LANES)
        ky = lax.broadcasted_iota(jnp.int32, shape, 0) + first_wavenumber()
        kx = lax.broadcasted_iota(jnp.int32, shape, 1) + block * LANES
        fold_x = jnp.minimum(kx, NX - kx).astype(jnp.float32) * (2.0 / NX)
        fold_y = jnp.minimum(ky, NY - ky).astype(jnp.float32) * (2.0 / NY)
        wave = jnp.sqrt(fold_x * fold_x + fold_y * fold_y)
        waves[:, lanes] = wave
        cosines[1, :, lanes] = jnp.cos(3.0 * wave)

    copies[0].wait()
    for group in range(groups):
        copies[group + 1].wait()

        @pl.loop(0, NX // LANES)
        def _(block):
            lanes = pl.ds(pl.multiple_of(block * LANES, LANES), LANES)
            now = cosines[1, :, lanes]
            double = now + now
            if group == 0:
                cosines[0, :, lanes] = double
                before = jnp.ones(shape, jnp.float32)
                real = jnp.zeros(shape, jnp.float32)
                imag = jnp.zeros(shape, jnp.float32)
            else:
                double = cosines[0, :, lanes]
                before = previous[:, lanes]
                real = total[0, :, lanes]
                imag = total[1, :, lanes]
            count = windows[:, lanes]
            for lag in range(group * LAGS + 1, group * LAGS + LAGS + 1):
                if lag > 1:
                    before, now = now, double * now - before
                weight = jnp.where(count >= lag, now * (2.0 * HIST + 2.0 - lag), 0.0)
                real = real + weight * stored[lag - 1, 0, :, lanes].astype(jnp.float32)
                imag = imag + weight * stored[lag - 1, 1, :, lanes].astype(jnp.float32)
            if group == groups - 1:
                factor = (waves[:, lanes] + 0.25) * (-0.5 / (2.0 * HIST + 2.0))
                real = real * factor
                imag = imag * factor
            else:
                cosines[1, :, lanes] = now
                previous[:, lanes] = before
            total[0, :, lanes] = real
            total[1, :, lanes] = imag

    for copy in copies[groups + 1 :]:
        copy.wait()

    @pl.loop(0, 8)
    def _(block):
        rows = pl.ds(pl.multiple_of(block * 64, 64), 64)
        velocity, strength = cells[0, rows, :], cells[2, rows, :]
        half_gain = 0.5 * jnp.exp(cells[3, rows, :])
        scaled = velocity * half_gain
        square = 1.0 + scaled * scaled
        root = square * lax.rsqrt(square)
        magnitude = jnp.log(jnp.abs(scaled) + root)
        stress = strength * jnp.where(scaled < 0, -magnitude, magnitude) + damping * velocity
        start[rows, :] = stress - cells[1, rows, :]
        inverse[rows, :] = root / (strength * half_gain + damping * root)


def modes_kernel(
    arrived,
    summed,
    waves,
    turn_in,
    turn_out,
    into,
    back,
    nyquist_wave,
    spectrum_out,
    out,
    left,
    mid,
    spec,
    gathered,
    spectrum,
    turned,
    sem,
):
    for part in range(2):
        lanes = slice(part * 128, part * 128 + 128)
        for piece in range(4):
            tile = arrived[pl.ds(part * 4 + piece, 128, stride=12), :]
            left[piece * 128 : piece * 128 + 128, lanes] = tile.T
        for piece in range(2):
            tile = arrived[pl.ds(8 + part * 2 + piece, 128, stride=12), :]
            left[512 + piece * 128 : 640 + piece * 128, lanes] = tile.T
    weights = (into[0], into[1])
    for piece in range(3):
        rows = pl.ds(piece * 256, 256)
        mid[rows, :] = exact_dot(split(left[rows, :]), weights)
    for f, half, first, stride in [(1, 0, 0, 16), (1, 1, 8, 16), (0, 0, 512, 8)]:
        for i1 in range(4):
            values = []
            for i2 in range(8):
                i = i1 + 4 * i2
                rows = slice(first + i * stride, first + i * stride + 8)
                values.append(times((mid[rows, 0:128], mid[rows, 128:256]), turn_in, i))
            for b1, value in enumerate(butterfly(values, -1)):
                value = turn(value, i1 * b1, 32, -1)
                spec[0, i1 * 8 + b1] = value[0]
                spec[1, i1 * 8 + b1] = value[1]
        for b1 in range(8):
            values = [(spec[0, i1 * 8 + b1], spec[1, i1 * 8 + b1]) for i1 in range(4)]
            for b2, value in enumerate(butterfly(values, -1)):
                b = b1 + 8 * b2
                for part in range(2):
                    rows = slice(half * 8, half * 8 + 8)
                    lanes = slice(b * 128, b * 128 + 128)
                    if f == 1:
                        spectrum[part, rows, lanes] = value[part]
                    else:
                        gathered[part, :, lanes] = value[part]
        if f == 1 and half == 1:
            finished = pltpu.make_async_copy(spectrum, spectrum_out, sem)
            finished.start()
    sublane = lax.broadcasted_iota(jnp.int32, (8, 128), 0)
    first = first_wavenumber()
    share_zero = jnp.where(first == 0, -0.5, jnp.where(first < NY // 2, -1.0, 0.0))
    share_eight = jnp.where(first < NY // 2, 0.0, -1.0)
    shares = (jnp.where(sublane == 0, share_zero, -1.0), jnp.where(sublane == 0, share_eight, 0.0))
    for half in range(3):
        rows = slice(half * 8, half * 8 + 8)
        for b1 in range(8):
            values = []
            for b2 in range(4):
                b = b1 + 8 * b2
                lanes = slice(b * 128, b * 128 + 128)
                if half == 2:
                    weight = nyquist_wave[b : b + 1, :] * -0.5
                    values.append(
                        tuple(
                            jnp.broadcast_to(gathered[part, 0:1, lanes] * weight, (8, 128))
                            for part in range(2)
                        )
                    )
                    continue
                wave = waves[rows, lanes]
                slip_weight = shares[half] * wave
                rate_weight = -0.5 * (wave + 0.25)
                values.append(
                    tuple(
                        slip_weight * gathered[part, :, lanes]
                        + rate_weight * spectrum[part, rows, lanes]
                        + summed[part, rows, lanes]
                        for part in range(2)
                    )
                )
            for i1, value in enumerate(butterfly(values, 1)):
                value = turn(value, i1 * b1, 32, 1)
                spec[0, i1 * 8 + b1] = value[0]
                spec[1, i1 * 8 + b1] = value[1]
        for i1 in range(4):
            values = [(spec[0, i1 * 8 + b1], spec[1, i1 * 8 + b1]) for b1 in range(8)]
            for i2, value in enumerate(butterfly(values, 1)):
                i = i1 + 4 * i2
                value = times(value, turn_out, i)
                start = (i // 8) * 128 + half * 64 + i % 8
                for part in range(2):
                    if half == 2:
                        turned[part, 512 + i : 513 + i, :] = value[part][0:1, :]
                    else:
                        turned[part, pl.ds(start, 8, stride=8), :] = value[part]
    weights = (back[0], back[1])

    def transform(rows, weights):
        lines = jnp.concatenate((turned[0, rows, :], turned[1, rows, :]), axis=1)
        return exact_dot(split(lines), weights)

    nyquist = transform(pl.ds(512, 128), (back[0, :, 128:256], back[1, :, 128:256])).T
    lane = lax.broadcasted_iota(jnp.int32, (128, 128), 1)
    for chunk in range(2):
        result = transform(pl.ds(chunk * 256, 256), weights)
        for part in range(2):
            for piece in range(2):
                tile = result[piece * 128 : piece * 128 + 128, part * 128 : part * 128 + 128].T
                group = chunk * 2 + piece
                if part == 1:
                    moved = pltpu.roll(nyquist, (128 - 8 * group) % 128, 1)
                    tile = jnp.where((lane < 8) & (first == 0), moved, tile)
                out[pl.ds(part * 4 + group, 128, stride=8), :] = tile
    finished.wait()


def cells_kernel(arrived, table, matrix, out, left):
    for piece in range(4):
        for part in range(2):
            tile = arrived[pl.ds(part * 4 + piece, 128, stride=8), :]
            left[piece * 128 : piece * 128 + 128, part * 128 : part * 128 + 128] = tile.T
    edges = [left[piece * 128 : piece * 128 + 8, 128:129] for piece in range(4)]
    parity = lax.broadcasted_iota(jnp.int32, (8, 128), 1) % 2
    alternating = jnp.where(parity == 0, 1.0, -1.0) * (0.5 / math.sqrt(NY))
    weights = (matrix[0], matrix[1])
    for chunk in range(2):
        rows = pl.ds(chunk * 256, 256)
        left[rows, :] = exact_dot(split(left[rows, :]), weights)
    for piece in range(4):
        values = []
        for k in range(16):
            row = piece * 128 + k * 8
            value = (left[row : row + 8, 0:128], left[row : row + 8, 128:256])
            values.append(times(value, table, k))
        constant = values[0][0] + alternating * edges[piece]
        modes = [(constant + constant, None)]
        modes += [add(values[k], conj(values[16 - k])) for k in range(1, 8)]
        modes += [(values[8][0] + values[8][0], None)]
        for c, value in enumerate(real_inverse(modes)):
            out[c, piece * 8 : piece * 8 + 8, :] = value


def call(kernel, out_shape, scratch, flops, **extra):
    return pl.pallas_call(
        kernel,
        out_shape=out_shape,
        scratch_shapes=scratch,
        compiler_params=pltpu.CompilerParams(vmem_limit_bytes=VMEM_LIMIT),
        cost_estimate=pl.CostEstimate(flops=flops, bytes_accessed=4 << 20, transcendentals=0),
        **extra,
    )


def f32(*shape):
    return jax.ShapeDtypeStruct(shape, jnp.float32)


def early_work(*arrays):
    return pl.pallas_call(
        early_kernel,
        in_specs=[pl.BlockSpec(memory_space=pl.ANY)] * 6,
        out_shape=[f32(2, 16, NX), f32(16, NX), f32(512, 128), f32(512, 128)],
        scratch_shapes=[
            pltpu.VMEM((HIST, 2, 16, NX), jnp.bfloat16),
            pltpu.VMEM((16, NX), jnp.int32),
            pltpu.VMEM((4, 512, 128), jnp.float32),
            pltpu.VMEM((2, 16, NX), jnp.float32),
            pltpu.VMEM((16, NX), jnp.float32),
            pltpu.SemaphoreType.DMA((HIST // LAGS + 5,)),
        ],
        compiler_params=pltpu.CompilerParams(vmem_limit_bytes=VMEM_LIMIT),
        cost_estimate=pl.CostEstimate(
            flops=40_000_000, bytes_accessed=10 << 20, transcendentals=3 * 65536
        ),
    )(*(pltpu.with_memory_space_constraint(array, pltpu.HBM) for array in arrays))


def on_device(slip, slip_rate, loading, friction, state, history, windows):
    everyone = ("rows", "cols")
    scratch = lambda *shape: pltpu.VMEM(shape, jnp.float32)
    whole = pl.BlockSpec(memory_space=pltpu.VMEM)
    remote = pl.BlockSpec(memory_space=pl.ANY)
    cells = jnp.stack((slip.reshape(16, 32, 128), slip_rate.reshape(16, 32, 128)), 1)
    lines = lax.all_to_all(cells, "cols", split_axis=0, concat_axis=0, tiled=True)

    summed, waves, start, inverse = early_work(
        history, windows, slip_rate, loading, friction, state
    )

    outbound = call(
        lines_kernel,
        f32(1536, 128),
        [scratch(2, 1024, 128)],
        400_000_000,
        in_specs=[whole] * 3 + [remote],
    )(lines, twiddle(16, NY, -1), dft_matrix(-1, 1.0 / math.sqrt(NY), True), waves)
    arrived = lax.all_to_all(
        outbound.reshape(128, 12 * 128), everyone, split_axis=0, concat_axis=0, tiled=True
    ).reshape(1536, 128)
    spectrum, outgoing = call(
        modes_kernel,
        [f32(2, 16, NX), f32(1024, 128)],
        [
            scratch(768, 256),
            scratch(768, 256),
            scratch(2, 32, 8, 128),
            scratch(2, 8, NX),
            scratch(2, 16, NX),
            scratch(2, 640, 128),
            pltpu.SemaphoreType.DMA,
        ],
        600_000_000,
        in_specs=[whole] * 8,
        out_specs=[remote, whole],
    )(
        arrived,
        summed,
        waves,
        twiddle(32, NX, -1),
        twiddle(32, NX, 1),
        dft_matrix(-1, 1.0 / math.sqrt(NX), False),
        dft_matrix(1, 1.0 / math.sqrt(NX), False),
        nyquist_waves(),
    )
    returned = lax.all_to_all(
        outgoing.reshape(128, 8, 128), everyone, split_axis=0, concat_axis=0, tiled=True
    ).reshape(1024, 128)
    stress = call(cells_kernel, f32(16, 32, 128), [scratch(512, 256)], 200_000_000)(
        returned, twiddle(16, NY, 1), dft_matrix(1, 0.5 / math.sqrt(NY), False)
    )
    transfer = lax.all_to_all(stress, "cols", split_axis=0, concat_axis=0, tiled=True)
    transfer = transfer.reshape(512, 128)

    traction = loading + transfer
    half_gain = 0.5 * jnp.exp(state)
    steepness = friction * half_gain
    velocity = slip_rate - (start - transfer) * inverse
    for sweep in range(NEWTON - 1):
        scaled = velocity * half_gain
        square = 1.0 + scaled * scaled
        root = square * lax.rsqrt(square)
        magnitude = jnp.log(jnp.abs(scaled) + root)
        mismatch = friction * jnp.where(scaled < 0, -magnitude, magnitude) + damping * velocity - traction
        velocity = velocity - mismatch * root / (steepness + damping * root)
    return (velocity, traction - damping * velocity, spectrum)


def solution(mesh):
    cell = P("rows", "cols")
    placed = (cell,) * 5 + (P(None, None, ("rows", "cols"), None), P(("rows", "cols"), None))
    return jax.shard_map(
        on_device,
        mesh=mesh,
        in_specs=placed,
        out_specs=(cell, cell, P(None, ("rows", "cols"), None)),
        check_vma=False,
    )
```

```python
import functools
import math

import jax
import jax.numpy as jnp
import ml_dtypes
import numpy as np
from jax import lax
from jax.experimental import pallas as pl
from jax.experimental.pallas import tpu as pltpu
from jax.sharding import PartitionSpec as P

NX = 4096
NY = 2048
HIST = 32
NEWTON = 3
damping = 1.0
LANES = 512
LAGS = 4
VMEM_LIMIT = 24 * 1024 * 1024


def split_host(matrix):
    full = matrix.astype(np.float32)
    high = full.astype(ml_dtypes.bfloat16)
    low = (full - high.astype(np.float32)).astype(ml_dtypes.bfloat16)
    return np.stack((high, low))


def dft_matrix(sign, scale, transposed):
    index = np.arange(128)
    phase = sign * 2.0 * math.pi * (np.outer(index, index) % 128) / 128.0
    cos, sin = np.cos(phase) * scale, np.sin(phase) * scale
    matrix = np.block([[cos, sin], [-sin, cos]])
    return split_host(matrix.T if transposed else matrix)


def twiddle(count, length, sign):
    phase = sign * 2.0 * math.pi * np.outer(np.arange(count), np.arange(128)) / length
    return np.stack((np.cos(phase), np.sin(phase))).astype(np.float32)


def constant_waves():
    kx = np.arange(NX, dtype=np.float32)
    fold = np.minimum(kx, NX - kx) * np.float32(2.0 / NX)
    return fold.reshape(32, 128)


def add(a, b):
    return (a[0] + b[0], a[1] + b[1])


def sub(a, b):
    return (a[0] - b[0], a[1] - b[1])


def conj(a):
    return (a[0], -a[1])


def turn(value, numerator, length, sign):
    numerator %= length
    re, im = value
    if numerator == 0:
        return value
    if 4 * numerator == length:
        return (-im, re) if sign > 0 else (im, -re)
    if 2 * numerator == length:
        return (-re, -im)
    if 4 * numerator == 3 * length:
        return (im, -re) if sign > 0 else (-im, re)
    if 8 * numerator % length == 0:
        half = math.sqrt(0.5)
        octant = 8 * numerator // length
        cos_sign = 1.0 if octant in (1, 7) else -1.0
        sin_sign = (1.0 if octant in (1, 3) else -1.0) * sign
        first = re if cos_sign > 0 else -re
        second = im if cos_sign > 0 else -im
        if sin_sign > 0:
            return ((first - im) * half, (re + second) * half)
        return ((first + im) * half, (second - re) * half)
    angle = 2.0 * math.pi * numerator / length
    cos, sin = math.cos(angle), sign * math.sin(angle)
    return (re * cos - im * sin, re * sin + im * cos)


def butterfly(values, sign):
    size = len(values)
    if size == 1:
        return values
    even = butterfly(values[0::2], sign)
    odd = butterfly(values[1::2], sign)
    turned = [turn(odd[k], k, size, sign) for k in range(size // 2)]
    return [add(e, t) for e, t in zip(even, turned)] + [sub(e, t) for e, t in zip(even, turned)]


def real_forward(values):
    size = len(values)
    if size == 2:
        return [(values[0] + values[1], None), (values[0] - values[1], None)]
    even = real_forward(values[0::2])
    odd = real_forward(values[1::2])
    quarter = size // 4
    out = [None] * (size // 2 + 1)
    for k in range(quarter + 1):
        e, o = even[k], odd[k]
        if k == 0:
            out[0] = (e[0] + o[0], None)
            out[size // 2] = (e[0] - o[0], None)
        elif k == quarter:
            out[k] = (e[0], -o[0])
        else:
            t = turn(o, k, size, -1)
            out[k] = add(e, t)
            out[size // 2 - k] = conj(sub(e, t))
    return out


def real_inverse(modes):
    half = len(modes) - 1
    size = 2 * half
    if size == 2:
        return [modes[0][0] + modes[1][0], modes[0][0] - modes[1][0]]
    quarter = half // 2
    even, odd = [], []
    for k in range(quarter + 1):
        a, b = modes[k], modes[half - k]
        if k == 0:
            even.append((a[0] + b[0], None))
            odd.append((a[0] - b[0], None))
        elif k == quarter:
            even.append((a[0] + a[0], None))
            odd.append((-(a[1] + a[1]), None))
        else:
            even.append(add(a, conj(b)))
            odd.append(turn(sub(a, conj(b)), k, size, 1))
    first, second = real_inverse(even), real_inverse(odd)
    out = []
    for e, o in zip(first, second):
        out += [e, o]
    return out


def times(value, table, index, rows=None):
    cos, sin = table[0, index : index + 1, :], table[1, index : index + 1, :]
    re, im = value
    if im is None:
        return (re * cos, re * sin)
    return (re * cos - im * sin, re * sin + im * cos)


def first_wavenumber():
    return lax.axis_index(("rows", "cols")) * 16


def split(value):
    high = value.astype(jnp.bfloat16)
    return high, (value - high.astype(jnp.float32)).astype(jnp.bfloat16)


def dot(left, right):
    return jnp.dot(left, right, preferred_element_type=jnp.float32)


def dot_transposed(left, right):
    return lax.dot_general(
        left, right, (((1,), (1,)), ((), ())), preferred_element_type=jnp.float32
    )


def exact_dot(data, matrix):
    (high, low), (matrix_high, matrix_low) = data, matrix
    count = matrix_high.shape[1]
    wide = dot(high, jnp.concatenate((matrix_high, matrix_low), axis=1))
    return wide[:, :count] + (wide[:, count:] + dot(low, matrix_high))


def gather_kernel(slip, slip_rate, cells, held, sems):
    fields = (slip, slip_rate)
    reads = [pltpu.make_async_copy(fields[f], held.at[f], sems.at[f]) for f in range(2)]
    writes = [pltpu.make_async_copy(held.at[f], cells.at[:, f], sems.at[2 + f]) for f in range(2)]
    for read in reads:
        read.start()
    for read, write in zip(reads, writes):
        read.wait()
        write.start()
    for write in writes:
        write.wait()


def lines_kernel(cells, table, matrix, unused, out, work):
    del unused
    for f in range(2):
        for group in range(4):
            samples = [cells[c, f, 8 * group : 8 * group + 8, :] for c in range(16)]
            modes = real_forward(samples)
            for k in range(16 if f == 1 else 9):
                value = times(modes[k] if k <= 8 else conj(modes[16 - k]), table, k)
                if f == 1:
                    places = [pl.ds(group * 128 + k, 8, stride=16)]
                elif k < 8:
                    places = [pl.ds(512 + group * 64 + k, 8, stride=8)]
                else:
                    places = [pl.ds(768 + group * 64 + slot, 8, stride=8) for slot in range(8)]
                for rows in places:
                    work[0, rows, :] = value[0]
                    work[1, rows, :] = value[1]
    weights = (matrix[0], matrix[1])

    def transform(chunk):
        rows = pl.ds(chunk * 256, 256)
        turned = jnp.concatenate((work[0, rows, :], work[1, rows, :]), axis=1)
        high, low = split(turned)
        return dot_transposed(weights[0], high) + (
            dot_transposed(weights[1], high) + dot_transposed(weights[0], low)
        )

    def tile_of(result, part, piece):
        return result[part * 128 : part * 128 + 128, piece * 128 : piece * 128 + 128]

    for chunk in range(2):
        result = transform(chunk)
        for part in range(2):
            for piece in range(2):
                out[pl.ds(part * 4 + chunk * 2 + piece, 128, stride=12), :] = tile_of(
                    result, part, piece
                )
    lower, upper = transform(2), transform(3)
    owner = lax.broadcasted_iota(jnp.int32, (128, 128), 0)
    first_slot = lax.broadcasted_iota(jnp.int32, (128, 128), 1) % 8 == 0
    for part in range(2):
        for piece in range(2):
            tile = jnp.where(
                first_slot & (owner < 64), tile_of(upper, part, piece), tile_of(lower, part, piece)
            )
            if part == 1:
                constant = lower[0:1, piece * 128 : piece * 128 + 128]
                tile = jnp.where(first_slot & (owner == 64), constant, tile)
            out[pl.ds(8 + part * 2 + piece, 128, stride=12), :] = tile


def early_kernel(
    history, counts, rate, loading, friction, state, total, waves, start, inverse, stored, windows, cells, cosines, previous, sems
):
    groups = HIST // LAGS
    copies = [pltpu.make_async_copy(counts, windows, sems.at[groups])]
    for group in range(groups):
        lags = pl.ds(group * LAGS, LAGS)
        copies.append(pltpu.make_async_copy(history.at[lags], stored.at[lags], sems.at[group]))
    for index, field in enumerate((rate, loading, friction, state)):
        copies.append(pltpu.make_async_copy(field, cells.at[index], sems.at[groups + 1 + index]))
    for copy in copies:
        copy.start()
    shape = (16, LANES)

    @pl.loop(0, NX // LANES)
    def _(block):
        lanes = pl.ds(pl.multiple_of(block * LANES, LANES), LANES)
        ky = lax.broadcasted_iota(jnp.int32, shape, 0) + first_wavenumber()
        kx = lax.broadcasted_iota(jnp.int32, shape, 1) + block * LANES
        fold_x = jnp.minimum(kx, NX - kx).astype(jnp.float32) * (2.0 / NX)
        fold_y = jnp.minimum(ky, NY - ky).astype(jnp.float32) * (2.0 / NY)
        wave = jnp.sqrt(fold_x * fold_x + fold_y * fold_y)
        waves[:, lanes] = wave
        cosines[1, :, lanes] = jnp.cos(3.0 * wave)

    copies[0].wait()
    for group in range(groups):
        copies[group + 1].wait()

        @pl.loop(0, NX // LANES)
        def _(block):
            lanes = pl.ds(pl.multiple_of(block * LANES, LANES), LANES)
            now = cosines[1, :, lanes]
            double = now + now
            if group == 0:
                cosines[0, :, lanes] = double
                before = jnp.ones(shape, jnp.float32)
                real = jnp.zeros(shape, jnp.float32)
                imag = jnp.zeros(shape, jnp.float32)
            else:
                double = cosines[0, :, lanes]
                before = previous[:, lanes]
                real = total[0, :, lanes]
                imag = total[1, :, lanes]
            count = windows[:, lanes]
            for lag in range(group * LAGS + 1, group * LAGS + LAGS + 1):
                if lag > 1:
                    before, now = now, double * now - before
                weight = jnp.where(count >= lag, now * (2.0 * HIST + 2.0 - lag), 0.0)
                real = real + weight * stored[lag - 1, 0, :, lanes].astype(jnp.float32)
                imag = imag + weight * stored[lag - 1, 1, :, lanes].astype(jnp.float32)
            if group == groups - 1:
                factor = (waves[:, lanes] + 0.25) * (-0.5 / (2.0 * HIST + 2.0))
                real = real * factor
                imag = imag * factor
            else:
                cosines[1, :, lanes] = now
                previous[:, lanes] = before
            total[0, :, lanes] = real
            total[1, :, lanes] = imag

    for copy in copies[groups + 1 :]:
        copy.wait()

    @pl.loop(0, 8)
    def _(block):
        rows = pl.ds(pl.multiple_of(block * 64, 64), 64)
        velocity, strength = cells[0, rows, :], cells[2, rows, :]
        half_gain = 0.5 * jnp.exp(cells[3, rows, :])
        scaled = velocity * half_gain
        square = 1.0 + scaled * scaled
        root = square * lax.rsqrt(square)
        magnitude = jnp.log(jnp.abs(scaled) + root)
        stress = strength * jnp.where(scaled < 0, -magnitude, magnitude) + damping * velocity
        start[rows, :] = stress - cells[1, rows, :]
        inverse[rows, :] = root / (strength * half_gain + damping * root)


def modes_kernel(
    arrived,
    summed,
    waves,
    turn_in,
    turn_out,
    into,
    back,
    constant_wave,
    spectrum_out,
    out,
    left,
    mid,
    spec,
    gathered,
    spectrum,
    turned,
    sem,
):
    for part in range(2):
        lanes = slice(part * 128, part * 128 + 128)
        for piece in range(4):
            tile = arrived[pl.ds(part * 4 + piece, 128, stride=12), :]
            left[piece * 128 : piece * 128 + 128, lanes] = tile.T
        for piece in range(2):
            tile = arrived[pl.ds(8 + part * 2 + piece, 128, stride=12), :]
            left[512 + piece * 128 : 640 + piece * 128, lanes] = tile.T
    weights = (into[0], into[1])
    for piece in range(3):
        rows = pl.ds(piece * 256, 256)
        mid[rows, :] = exact_dot(split(left[rows, :]), weights)
    for f, half, first, stride in [(1, 0, 0, 16), (1, 1, 8, 16), (0, 0, 512, 8)]:
        for i1 in range(4):
            values = []
            for i2 in range(8):
                i = i1 + 4 * i2
                rows = slice(first + i * stride, first + i * stride + 8)
                values.append(times((mid[rows, 0:128], mid[rows, 128:256]), turn_in, i))
            for b1, value in enumerate(butterfly(values, -1)):
                value = turn(value, i1 * b1, 32, -1)
                spec[0, i1 * 8 + b1] = value[0]
                spec[1, i1 * 8 + b1] = value[1]
        for b1 in range(8):
            values = [(spec[0, i1 * 8 + b1], spec[1, i1 * 8 + b1]) for i1 in range(4)]
            for b2, value in enumerate(butterfly(values, -1)):
                b = b1 + 8 * b2
                for part in range(2):
                    rows = slice(half * 8, half * 8 + 8)
                    lanes = slice(b * 128, b * 128 + 128)
                    if f == 1:
                        spectrum[part, rows, lanes] = value[part]
                    else:
                        gathered[part, :, lanes] = value[part]
        if f == 1 and half == 1:
            finished = pltpu.make_async_copy(spectrum, spectrum_out, sem)
            finished.start()
    sublane = lax.broadcasted_iota(jnp.int32, (8, 128), 0)
    first = first_wavenumber()
    share_zero = jnp.where(first == NY // 2, -0.5, jnp.where(first < NY // 2, 0.0, -1.0))
    share_eight = jnp.where(first < NY // 2, -1.0, 0.0)
    shares = (jnp.where(sublane == 0, share_zero, -1.0), jnp.where(sublane == 0, share_eight, 0.0))
    for half in range(2):
        rows = slice(half * 8, half * 8 + 8)
        for b1 in range(8):
            values = []
            for b2 in range(4):
                b = b1 + 8 * b2
                lanes = slice(b * 128, b * 128 + 128)
                wave = waves[rows, lanes]
                slip_weight = shares[half] * wave
                rate_weight = -0.5 * (wave + 0.25)
                values.append(
                    tuple(
                        slip_weight * gathered[part, :, lanes]
                        + rate_weight * spectrum[part, rows, lanes]
                        + summed[part, rows, lanes]
                        for part in range(2)
                    )
                )
            for i1, value in enumerate(butterfly(values, 1)):
                value = turn(value, i1 * b1, 32, 1)
                spec[0, i1 * 8 + b1] = value[0]
                spec[1, i1 * 8 + b1] = value[1]
        for i1 in range(4):
            values = [(spec[0, i1 * 8 + b1], spec[1, i1 * 8 + b1]) for b1 in range(8)]
            for i2, value in enumerate(butterfly(values, 1)):
                i = i1 + 4 * i2
                value = times(value, turn_out, i)
                start = (i // 8) * 128 + half * 64 + i % 8
                for part in range(2):
                    turned[part, pl.ds(start, 8, stride=8), :] = value[part]
    weights = (back[0], back[1])

    def transform(rows, weights):
        lines = jnp.concatenate((turned[0, rows, :], turned[1, rows, :]), axis=1)
        return exact_dot(split(lines), weights)

    for chunk in range(2):
        result = transform(pl.ds(chunk * 256, 256), weights)
        for part in range(2):
            for piece in range(2):
                tile = result[piece * 128 : piece * 128 + 128, part * 128 : part * 128 + 128].T
                group = chunk * 2 + piece
                out[pl.ds(part * 4 + group, 128, stride=8), :] = tile

    @pl.when(first == NY // 2)
    def _():
        for b1 in range(8):
            values = []
            for b2 in range(4):
                b = b1 + 8 * b2
                weight = constant_wave[b : b + 1, :] * -0.5
                values.append(
                    tuple(
                        jnp.broadcast_to(
                            gathered[part, 0:1, b * 128 : b * 128 + 128] * weight, (8, 128)
                        )
                        for part in range(2)
                    )
                )
            for i1, value in enumerate(butterfly(values, 1)):
                value = turn(value, i1 * b1, 32, 1)
                spec[0, i1 * 8 + b1] = value[0]
                spec[1, i1 * 8 + b1] = value[1]
        for i1 in range(4):
            values = [(spec[0, i1 * 8 + b1], spec[1, i1 * 8 + b1]) for b1 in range(8)]
            for i2, value in enumerate(butterfly(values, 1)):
                i = i1 + 4 * i2
                value = times(value, turn_out, i)
                for part in range(2):
                    turned[part, i : i + 1, :] = value[part][0:1, :]
        constant = transform(pl.ds(0, 128), (back[0, :, 128:256], back[1, :, 128:256])).T
        lane = lax.broadcasted_iota(jnp.int32, (128, 128), 1)
        for group in range(4):
            rows = pl.ds(4 + group, 128, stride=8)
            moved = pltpu.roll(constant, (128 - 8 * group) % 128, 1)
            out[rows, :] = jnp.where(lane < 8, moved, out[rows, :])

    finished.wait()


def cells_kernel(arrived, table, matrix, out, left):
    for piece in range(4):
        for part in range(2):
            tile = arrived[pl.ds(part * 4 + piece, 128, stride=8), :]
            left[piece * 128 : piece * 128 + 128, part * 128 : part * 128 + 128] = tile.T
    means = [left[piece * 128 : piece * 128 + 8, 192:193] for piece in range(4)]
    weights = (matrix[0], matrix[1])
    for chunk in range(2):
        rows = pl.ds(chunk * 256, 256)
        left[rows, :] = exact_dot(split(left[rows, :]), weights)
    for piece in range(4):
        values = []
        for k in range(16):
            row = piece * 128 + k * 8
            value = (left[row : row + 8, 0:128], left[row : row + 8, 128:256])
            values.append(times(value, table, k))
        constant = values[0][0] + means[piece] * (0.5 / math.sqrt(NY))
        modes = [(constant + constant, None)]
        modes += [add(values[k], conj(values[16 - k])) for k in range(1, 8)]
        modes += [(values[8][0] + values[8][0], None)]
        for c, value in enumerate(real_inverse(modes)):
            out[c, piece * 8 : piece * 8 + 8, :] = value


def call(kernel, out_shape, scratch, flops, **extra):
    return pl.pallas_call(
        kernel,
        out_shape=out_shape,
        scratch_shapes=scratch,
        compiler_params=pltpu.CompilerParams(vmem_limit_bytes=VMEM_LIMIT),
        cost_estimate=pl.CostEstimate(flops=flops, bytes_accessed=4 << 20, transcendentals=0),
        **extra,
    )


def f32(*shape):
    return jax.ShapeDtypeStruct(shape, jnp.float32)


def early_work(*arrays):
    return pl.pallas_call(
        early_kernel,
        in_specs=[pl.BlockSpec(memory_space=pl.ANY)] * 6,
        out_shape=[f32(2, 16, NX), f32(16, NX), f32(512, 128), f32(512, 128)],
        scratch_shapes=[
            pltpu.VMEM((HIST, 2, 16, NX), jnp.bfloat16),
            pltpu.VMEM((16, NX), jnp.int32),
            pltpu.VMEM((4, 512, 128), jnp.float32),
            pltpu.VMEM((2, 16, NX), jnp.float32),
            pltpu.VMEM((16, NX), jnp.float32),
            pltpu.SemaphoreType.DMA((HIST // LAGS + 5,)),
        ],
        compiler_params=pltpu.CompilerParams(vmem_limit_bytes=VMEM_LIMIT),
        cost_estimate=pl.CostEstimate(
            flops=40_000_000, bytes_accessed=10 << 20, transcendentals=3 * 65536
        ),
    )(*(pltpu.with_memory_space_constraint(array, pltpu.HBM) for array in arrays))


def on_device(slip, slip_rate, loading, friction, state, history, windows):
    everyone = ("rows", "cols")
    scratch = lambda *shape: pltpu.VMEM(shape, jnp.float32)
    whole = pl.BlockSpec(memory_space=pltpu.VMEM)
    remote = pl.BlockSpec(memory_space=pl.ANY)
    remote = pl.BlockSpec(memory_space=pl.ANY)
    cells = pl.pallas_call(
        gather_kernel,
        in_specs=[remote] * 2,
        out_specs=remote,
        out_shape=pltpu.HBM((16, 2, 32, 128), jnp.float32),
        scratch_shapes=[
            pltpu.VMEM((2, 16, 32, 128), jnp.float32),
            pltpu.SemaphoreType.DMA((4,)),
        ],
    )(
        pltpu.with_memory_space_constraint(slip.reshape(16, 32, 128), pltpu.HBM),
        pltpu.with_memory_space_constraint(slip_rate.reshape(16, 32, 128), pltpu.HBM),
    )
    lines = lax.all_to_all(cells, "cols", split_axis=0, concat_axis=0, tiled=True)

    summed, waves, start, inverse = early_work(
        history, windows, slip_rate, loading, friction, state
    )

    outbound = call(
        lines_kernel,
        f32(1536, 128),
        [scratch(2, 1024, 128)],
        400_000_000,
        in_specs=[whole] * 3 + [remote],
    )(lines, twiddle(16, NY, -1), dft_matrix(-1, 1.0 / math.sqrt(NY), True), waves)
    arrived = lax.all_to_all(
        outbound.reshape(128, 12 * 128), everyone, split_axis=0, concat_axis=0, tiled=True
    ).reshape(1536, 128)
    spectrum, outgoing = call(
        modes_kernel,
        [f32(2, 16, NX), f32(1024, 128)],
        [
            scratch(768, 256),
            scratch(768, 256),
            scratch(2, 32, 8, 128),
            scratch(2, 8, NX),
            scratch(2, 16, NX),
            scratch(2, 512, 128),
            pltpu.SemaphoreType.DMA,
        ],
        600_000_000,
        in_specs=[whole] * 8,
        out_specs=[remote, whole],
    )(
        arrived,
        summed,
        waves,
        twiddle(32, NX, -1),
        twiddle(32, NX, 1),
        dft_matrix(-1, 1.0 / math.sqrt(NX), False),
        dft_matrix(1, 1.0 / math.sqrt(NX), False),
        constant_waves(),
    )
    returned = lax.all_to_all(
        outgoing.reshape(128, 8, 128), everyone, split_axis=0, concat_axis=0, tiled=True
    ).reshape(1024, 128)
    stress = call(cells_kernel, f32(16, 32, 128), [scratch(512, 256)], 200_000_000)(
        returned, twiddle(16, NY, 1), dft_matrix(1, 0.5 / math.sqrt(NY), False)
    )
    transfer = lax.all_to_all(stress, "cols", split_axis=0, concat_axis=0, tiled=True)
    transfer = transfer.reshape(512, 128)

    traction = loading + transfer
    half_gain = 0.5 * jnp.exp(state)
    steepness = friction * half_gain
    velocity = slip_rate - (start - transfer) * inverse
    for sweep in range(NEWTON - 1):
        scaled = velocity * half_gain
        square = 1.0 + scaled * scaled
        root = square * lax.rsqrt(square)
        magnitude = jnp.log(jnp.abs(scaled) + root)
        mismatch = friction * jnp.where(scaled < 0, -magnitude, magnitude) + damping * velocity - traction
        velocity = velocity - mismatch * root / (steepness + damping * root)
    return (velocity, traction - damping * velocity, spectrum)


def solution(mesh):
    cell = P("rows", "cols")
    placed = (cell,) * 5 + (P(None, None, ("rows", "cols"), None), P(("rows", "cols"), None))
    return jax.shard_map(
        on_device,
        mesh=mesh,
        in_specs=placed,
        out_specs=(cell, cell, P(None, ("rows", "cols"), None)),
        check_vma=False,
    )
```

```python
import functools
import math

import jax
import jax.numpy as jnp
import ml_dtypes
import numpy as np
from jax import lax
from jax.experimental import pallas as pl
from jax.experimental.pallas import tpu as pltpu
from jax.sharding import PartitionSpec as P

NX = 4096
NY = 2048
HIST = 32
NEWTON = 3
damping = 1.0
LANES = 512
LAGS = 4
VMEM_LIMIT = 24 * 1024 * 1024


def split_host(matrix):
    full = matrix.astype(np.float32)
    high = full.astype(ml_dtypes.bfloat16)
    low = (full - high.astype(np.float32)).astype(ml_dtypes.bfloat16)
    return np.stack((high, low))


def dft_matrix(sign, scale, transposed):
    index = np.arange(128)
    phase = sign * 2.0 * math.pi * (np.outer(index, index) % 128) / 128.0
    cos, sin = np.cos(phase) * scale, np.sin(phase) * scale
    matrix = np.block([[cos, sin], [-sin, cos]])
    return split_host(matrix.T if transposed else matrix)


def twiddle(count, length, sign):
    phase = sign * 2.0 * math.pi * np.outer(np.arange(count), np.arange(128)) / length
    return np.stack((np.cos(phase), np.sin(phase))).astype(np.float32)


def constant_waves():
    kx = np.arange(NX, dtype=np.float32)
    fold = np.minimum(kx, NX - kx) * np.float32(2.0 / NX)
    return fold.reshape(32, 128)


def add(a, b):
    return (a[0] + b[0], a[1] + b[1])


def sub(a, b):
    return (a[0] - b[0], a[1] - b[1])


def conj(a):
    return (a[0], -a[1])


def turn(value, numerator, length, sign):
    numerator %= length
    re, im = value
    if numerator == 0:
        return value
    if 4 * numerator == length:
        return (-im, re) if sign > 0 else (im, -re)
    if 2 * numerator == length:
        return (-re, -im)
    if 4 * numerator == 3 * length:
        return (im, -re) if sign > 0 else (-im, re)
    if 8 * numerator % length == 0:
        half = math.sqrt(0.5)
        octant = 8 * numerator // length
        cos_sign = 1.0 if octant in (1, 7) else -1.0
        sin_sign = (1.0 if octant in (1, 3) else -1.0) * sign
        first = re if cos_sign > 0 else -re
        second = im if cos_sign > 0 else -im
        if sin_sign > 0:
            return ((first - im) * half, (re + second) * half)
        return ((first + im) * half, (second - re) * half)
    angle = 2.0 * math.pi * numerator / length
    cos, sin = math.cos(angle), sign * math.sin(angle)
    return (re * cos - im * sin, re * sin + im * cos)


def butterfly(values, sign):
    size = len(values)
    if size == 1:
        return values
    even = butterfly(values[0::2], sign)
    odd = butterfly(values[1::2], sign)
    turned = [turn(odd[k], k, size, sign) for k in range(size // 2)]
    return [add(e, t) for e, t in zip(even, turned)] + [sub(e, t) for e, t in zip(even, turned)]


def real_forward(values):
    size = len(values)
    if size == 2:
        return [(values[0] + values[1], None), (values[0] - values[1], None)]
    even = real_forward(values[0::2])
    odd = real_forward(values[1::2])
    quarter = size // 4
    out = [None] * (size // 2 + 1)
    for k in range(quarter + 1):
        e, o = even[k], odd[k]
        if k == 0:
            out[0] = (e[0] + o[0], None)
            out[size // 2] = (e[0] - o[0], None)
        elif k == quarter:
            out[k] = (e[0], -o[0])
        else:
            t = turn(o, k, size, -1)
            out[k] = add(e, t)
            out[size // 2 - k] = conj(sub(e, t))
    return out


def real_inverse(modes):
    half = len(modes) - 1
    size = 2 * half
    if size == 2:
        return [modes[0][0] + modes[1][0], modes[0][0] - modes[1][0]]
    quarter = half // 2
    even, odd = [], []
    for k in range(quarter + 1):
        a, b = modes[k], modes[half - k]
        if k == 0:
            even.append((a[0] + b[0], None))
            odd.append((a[0] - b[0], None))
        elif k == quarter:
            even.append((a[0] + a[0], None))
            odd.append((-(a[1] + a[1]), None))
        else:
            even.append(add(a, conj(b)))
            odd.append(turn(sub(a, conj(b)), k, size, 1))
    first, second = real_inverse(even), real_inverse(odd)
    out = []
    for e, o in zip(first, second):
        out += [e, o]
    return out


def times(value, table, index, rows=None):
    cos, sin = table[0, index : index + 1, :], table[1, index : index + 1, :]
    re, im = value
    if im is None:
        return (re * cos, re * sin)
    return (re * cos - im * sin, re * sin + im * cos)


def first_wavenumber():
    return lax.axis_index(("rows", "cols")) * 16


def split(value):
    high = value.astype(jnp.bfloat16)
    return high, (value - high.astype(jnp.float32)).astype(jnp.bfloat16)


def dot(left, right):
    return jnp.dot(left, right, preferred_element_type=jnp.float32)


def dot_transposed(left, right):
    return lax.dot_general(
        left, right, (((1,), (1,)), ((), ())), preferred_element_type=jnp.float32
    )


def exact_dot(data, matrix):
    (high, low), (matrix_high, matrix_low) = data, matrix
    count = matrix_high.shape[1]
    wide = dot(high, jnp.concatenate((matrix_high, matrix_low), axis=1))
    return wide[:, :count] + (wide[:, count:] + dot(low, matrix_high))


def gather_kernel(slip, slip_rate, cells, held, sems):
    fields = (slip, slip_rate)
    reads = [pltpu.make_async_copy(fields[f], held.at[f], sems.at[f]) for f in range(2)]
    writes = [pltpu.make_async_copy(held.at[f], cells.at[:, f], sems.at[2 + f]) for f in range(2)]
    for read in reads:
        read.start()
    for read, write in zip(reads, writes):
        read.wait()
        write.start()
    for write in writes:
        write.wait()


def lines_kernel(cells, table, matrix, unused, out, work):
    del unused
    for f in range(2):
        for group in range(4):
            samples = [cells[c, f, 8 * group : 8 * group + 8, :] for c in range(16)]
            modes = real_forward(samples)
            for k in range(16 if f == 1 else 9):
                value = times(modes[k] if k <= 8 else conj(modes[16 - k]), table, k)
                if f == 1:
                    places = [pl.ds(group * 128 + k, 8, stride=16)]
                else:
                    places = [pl.ds(512 + group * 64 + k, 8, stride=8)] if k < 8 else []
                    if k > 0:
                        places.append(pl.ds(768 + group * 64 + k % 8, 8, stride=8))
                for rows in places:
                    work[0, rows, :] = value[0]
                    work[1, rows, :] = value[1]

    def transform(chunk, weights):
        rows = pl.ds(chunk * 256, 256)
        turned = jnp.concatenate((work[0, rows, :], work[1, rows, :]), axis=1)
        high, low = split(turned)
        return dot_transposed(weights[0], high) + (
            dot_transposed(weights[1], high) + dot_transposed(weights[0], low)
        )

    def rows_of(*ranges):
        return [
            jnp.concatenate([matrix[level, first:last] for first, last in ranges], axis=0)
            for level in range(2)
        ]

    for chunk in range(2):
        result = transform(chunk, (matrix[0], matrix[1]))
        for part in range(2):
            for piece in range(2):
                out[pl.ds(part * 4 + chunk * 2 + piece, 128, stride=12), :] = result[
                    part * 128 : part * 128 + 128, piece * 128 : piece * 128 + 128
                ]
    later = transform(2, rows_of((64, 128), (192, 256), (0, 16)))
    earlier = transform(3, rows_of((0, 64), (128, 192)))
    row = lax.broadcasted_iota(jnp.int32, (64, 128), 0)
    first_slot = lax.broadcasted_iota(jnp.int32, (64, 128), 1) % 8 == 0
    for part in range(2):
        for piece in range(2):
            lanes = slice(piece * 128, piece * 128 + 128)
            tile = later[part * 64 : part * 64 + 64, lanes]
            if part == 1:
                tile = jnp.where(first_slot & (row == 0), later[128:129, lanes], tile)
            tile = jnp.concatenate((earlier[part * 64 : part * 64 + 64, lanes], tile), axis=0)
            out[pl.ds(8 + part * 2 + piece, 128, stride=12), :] = tile


def early_kernel(
    history, counts, rate, loading, friction, state, total, waves, start, inverse, stored, windows, cells, cosines, previous, sems
):
    groups = HIST // LAGS
    copies = [pltpu.make_async_copy(counts, windows, sems.at[groups])]
    for group in range(groups):
        lags = pl.ds(group * LAGS, LAGS)
        copies.append(pltpu.make_async_copy(history.at[lags], stored.at[lags], sems.at[group]))
    for index, field in enumerate((rate, loading, friction, state)):
        copies.append(pltpu.make_async_copy(field, cells.at[index], sems.at[groups + 1 + index]))
    for copy in copies:
        copy.start()
    shape = (16, LANES)

    @pl.loop(0, NX // LANES)
    def _(block):
        lanes = pl.ds(pl.multiple_of(block * LANES, LANES), LANES)
        ky = lax.broadcasted_iota(jnp.int32, shape, 0) + first_wavenumber()
        kx = lax.broadcasted_iota(jnp.int32, shape, 1) + block * LANES
        fold_x = jnp.minimum(kx, NX - kx).astype(jnp.float32) * (2.0 / NX)
        fold_y = jnp.minimum(ky, NY - ky).astype(jnp.float32) * (2.0 / NY)
        wave = jnp.sqrt(fold_x * fold_x + fold_y * fold_y)
        waves[:, lanes] = wave
        cosines[1, :, lanes] = jnp.cos(3.0 * wave)

    copies[0].wait()
    for group in range(groups):
        copies[group + 1].wait()

        @pl.loop(0, NX // LANES)
        def _(block):
            lanes = pl.ds(pl.multiple_of(block * LANES, LANES), LANES)
            now = cosines[1, :, lanes]
            double = now + now
            if group == 0:
                cosines[0, :, lanes] = double
                before = jnp.ones(shape, jnp.float32)
                real = jnp.zeros(shape, jnp.float32)
                imag = jnp.zeros(shape, jnp.float32)
            else:
                double = cosines[0, :, lanes]
                before = previous[:, lanes]
                real = total[0, :, lanes]
                imag = total[1, :, lanes]
            count = windows[:, lanes]
            for lag in range(group * LAGS + 1, group * LAGS + LAGS + 1):
                if lag > 1:
                    before, now = now, double * now - before
                weight = jnp.where(count >= lag, now * (2.0 * HIST + 2.0 - lag), 0.0)
                real = real + weight * stored[lag - 1, 0, :, lanes].astype(jnp.float32)
                imag = imag + weight * stored[lag - 1, 1, :, lanes].astype(jnp.float32)
            if group == groups - 1:
                factor = (waves[:, lanes] + 0.25) * (-0.5 / (2.0 * HIST + 2.0))
                real = real * factor
                imag = imag * factor
            else:
                cosines[1, :, lanes] = now
                previous[:, lanes] = before
            total[0, :, lanes] = real
            total[1, :, lanes] = imag

    for copy in copies[groups + 1 :]:
        copy.wait()

    @pl.loop(0, 8)
    def _(block):
        rows = pl.ds(pl.multiple_of(block * 64, 64), 64)
        velocity, strength = cells[0, rows, :], cells[2, rows, :]
        half_gain = 0.5 * jnp.exp(cells[3, rows, :])
        scaled = velocity * half_gain
        square = 1.0 + scaled * scaled
        root = square * lax.rsqrt(square)
        magnitude = jnp.log(jnp.abs(scaled) + root)
        stress = strength * jnp.where(scaled < 0, -magnitude, magnitude) + damping * velocity
        start[rows, :] = stress - cells[1, rows, :]
        inverse[rows, :] = root / (strength * half_gain + damping * root)


def modes_kernel(
    arrived,
    summed,
    waves,
    turn_in,
    turn_out,
    into,
    back,
    constant_wave,
    spectrum_out,
    out,
    left,
    mid,
    spec,
    gathered,
    spectrum,
    turned,
    sem,
):
    for part in range(2):
        lanes = slice(part * 128, part * 128 + 128)
        for piece in range(4):
            tile = arrived[pl.ds(part * 4 + piece, 128, stride=12), :]
            left[piece * 128 : piece * 128 + 128, lanes] = tile.T
        for piece in range(2):
            tile = arrived[pl.ds(8 + part * 2 + piece, 128, stride=12), :]
            left[512 + piece * 128 : 640 + piece * 128, lanes] = tile.T
    weights = (into[0], into[1])
    for piece in range(3):
        rows = pl.ds(piece * 256, 256)
        mid[rows, :] = exact_dot(split(left[rows, :]), weights)
    for f, half, first, stride in [(1, 0, 0, 16), (1, 1, 8, 16), (0, 0, 512, 8)]:
        for i1 in range(4):
            values = []
            for i2 in range(8):
                i = i1 + 4 * i2
                rows = slice(first + i * stride, first + i * stride + 8)
                values.append(times((mid[rows, 0:128], mid[rows, 128:256]), turn_in, i))
            for b1, value in enumerate(butterfly(values, -1)):
                value = turn(value, i1 * b1, 32, -1)
                spec[0, i1 * 8 + b1] = value[0]
                spec[1, i1 * 8 + b1] = value[1]
        for b1 in range(8):
            values = [(spec[0, i1 * 8 + b1], spec[1, i1 * 8 + b1]) for i1 in range(4)]
            for b2, value in enumerate(butterfly(values, -1)):
                b = b1 + 8 * b2
                for part in range(2):
                    rows = slice(half * 8, half * 8 + 8)
                    lanes = slice(b * 128, b * 128 + 128)
                    if f == 1:
                        spectrum[part, rows, lanes] = value[part]
                    else:
                        gathered[part, :, lanes] = value[part]
        if f == 1 and half == 1:
            finished = pltpu.make_async_copy(spectrum, spectrum_out, sem)
            finished.start()
    sublane = lax.broadcasted_iota(jnp.int32, (8, 128), 0)
    first = first_wavenumber()
    share_zero = jnp.where(first == NY // 2, -0.5, jnp.where(first < NY // 2, 0.0, -1.0))
    share_eight = jnp.where(first < NY // 2, -1.0, 0.0)
    shares = (jnp.where(sublane == 0, share_zero, -1.0), jnp.where(sublane == 0, share_eight, 0.0))
    for half in range(2):
        rows = slice(half * 8, half * 8 + 8)
        for b1 in range(8):
            values = []
            for b2 in range(4):
                b = b1 + 8 * b2
                lanes = slice(b * 128, b * 128 + 128)
                wave = waves[rows, lanes]
                slip_weight = shares[half] * wave
                rate_weight = -0.5 * (wave + 0.25)
                values.append(
                    tuple(
                        slip_weight * gathered[part, :, lanes]
                        + rate_weight * spectrum[part, rows, lanes]
                        + summed[part, rows, lanes]
                        for part in range(2)
                    )
                )
            for i1, value in enumerate(butterfly(values, 1)):
                value = turn(value, i1 * b1, 32, 1)
                spec[0, i1 * 8 + b1] = value[0]
                spec[1, i1 * 8 + b1] = value[1]
        for i1 in range(4):
            values = [(spec[0, i1 * 8 + b1], spec[1, i1 * 8 + b1]) for b1 in range(8)]
            for i2, value in enumerate(butterfly(values, 1)):
                i = i1 + 4 * i2
                value = times(value, turn_out, i)
                start = (i // 8) * 128 + half * 64 + i % 8
                for part in range(2):
                    turned[part, pl.ds(start, 8, stride=8), :] = value[part]
    weights = (back[0], back[1])

    def transform(rows, weights):
        lines = jnp.concatenate((turned[0, rows, :], turned[1, rows, :]), axis=1)
        return exact_dot(split(lines), weights)

    for chunk in range(2):
        result = transform(pl.ds(chunk * 256, 256), weights)
        for part in range(2):
            for piece in range(2):
                tile = result[piece * 128 : piece * 128 + 128, part * 128 : part * 128 + 128].T
                group = chunk * 2 + piece
                out[pl.ds(part * 4 + group, 128, stride=8), :] = tile

    @pl.when(first == NY // 2)
    def _():
        for b1 in range(8):
            values = []
            for b2 in range(4):
                b = b1 + 8 * b2
                weight = constant_wave[b : b + 1, :] * -0.5
                values.append(
                    tuple(
                        jnp.broadcast_to(
                            gathered[part, 0:1, b * 128 : b * 128 + 128] * weight, (8, 128)
                        )
                        for part in range(2)
                    )
                )
            for i1, value in enumerate(butterfly(values, 1)):
                value = turn(value, i1 * b1, 32, 1)
                spec[0, i1 * 8 + b1] = value[0]
                spec[1, i1 * 8 + b1] = value[1]
        for i1 in range(4):
            values = [(spec[0, i1 * 8 + b1], spec[1, i1 * 8 + b1]) for b1 in range(8)]
            for i2, value in enumerate(butterfly(values, 1)):
                i = i1 + 4 * i2
                value = times(value, turn_out, i)
                for part in range(2):
                    turned[part, i : i + 1, :] = value[part][0:1, :]
        constant = transform(pl.ds(0, 128), (back[0, :, 128:256], back[1, :, 128:256])).T
        lane = lax.broadcasted_iota(jnp.int32, (128, 128), 1)
        for group in range(4):
            rows = pl.ds(4 + group, 128, stride=8)
            moved = pltpu.roll(constant, (128 - 8 * group) % 128, 1)
            out[rows, :] = jnp.where(lane < 8, moved, out[rows, :])

    finished.wait()


def cells_kernel(arrived, table, matrix, out, left):
    for piece in range(4):
        for part in range(2):
            tile = arrived[pl.ds(part * 4 + piece, 128, stride=8), :]
            left[piece * 128 : piece * 128 + 128, part * 128 : part * 128 + 128] = tile.T
    means = [left[piece * 128 : piece * 128 + 8, 192:193] for piece in range(4)]
    weights = (matrix[0], matrix[1])
    for chunk in range(2):
        rows = pl.ds(chunk * 256, 256)
        left[rows, :] = exact_dot(split(left[rows, :]), weights)
    for piece in range(4):
        values = []
        for k in range(16):
            row = piece * 128 + k * 8
            value = (left[row : row + 8, 0:128], left[row : row + 8, 128:256])
            values.append(times(value, table, k))
        constant = values[0][0] + means[piece] * (0.5 / math.sqrt(NY))
        modes = [(constant + constant, None)]
        modes += [add(values[k], conj(values[16 - k])) for k in range(1, 8)]
        modes += [(values[8][0] + values[8][0], None)]
        for c, value in enumerate(real_inverse(modes)):
            out[c, piece * 8 : piece * 8 + 8, :] = value


def call(kernel, out_shape, scratch, flops, **extra):
    return pl.pallas_call(
        kernel,
        out_shape=out_shape,
        scratch_shapes=scratch,
        compiler_params=pltpu.CompilerParams(vmem_limit_bytes=VMEM_LIMIT),
        cost_estimate=pl.CostEstimate(flops=flops, bytes_accessed=4 << 20, transcendentals=0),
        **extra,
    )


def f32(*shape):
    return jax.ShapeDtypeStruct(shape, jnp.float32)


def early_work(*arrays):
    return pl.pallas_call(
        early_kernel,
        in_specs=[pl.BlockSpec(memory_space=pl.ANY)] * 6,
        out_shape=[f32(2, 16, NX), f32(16, NX), f32(512, 128), f32(512, 128)],
        scratch_shapes=[
            pltpu.VMEM((HIST, 2, 16, NX), jnp.bfloat16),
            pltpu.VMEM((16, NX), jnp.int32),
            pltpu.VMEM((4, 512, 128), jnp.float32),
            pltpu.VMEM((2, 16, NX), jnp.float32),
            pltpu.VMEM((16, NX), jnp.float32),
            pltpu.SemaphoreType.DMA((HIST // LAGS + 5,)),
        ],
        compiler_params=pltpu.CompilerParams(vmem_limit_bytes=VMEM_LIMIT),
        cost_estimate=pl.CostEstimate(
            flops=40_000_000, bytes_accessed=10 << 20, transcendentals=3 * 65536
        ),
    )(*(pltpu.with_memory_space_constraint(array, pltpu.HBM) for array in arrays))


def on_device(slip, slip_rate, loading, friction, state, history, windows):
    everyone = ("rows", "cols")
    scratch = lambda *shape: pltpu.VMEM(shape, jnp.float32)
    whole = pl.BlockSpec(memory_space=pltpu.VMEM)
    remote = pl.BlockSpec(memory_space=pl.ANY)
    remote = pl.BlockSpec(memory_space=pl.ANY)
    cells = pl.pallas_call(
        gather_kernel,
        in_specs=[remote] * 2,
        out_specs=remote,
        out_shape=pltpu.HBM((16, 2, 32, 128), jnp.float32),
        scratch_shapes=[
            pltpu.VMEM((2, 16, 32, 128), jnp.float32),
            pltpu.SemaphoreType.DMA((4,)),
        ],
    )(
        pltpu.with_memory_space_constraint(slip.reshape(16, 32, 128), pltpu.HBM),
        pltpu.with_memory_space_constraint(slip_rate.reshape(16, 32, 128), pltpu.HBM),
    )
    lines = lax.all_to_all(cells, "cols", split_axis=0, concat_axis=0, tiled=True)

    summed, waves, start, inverse = early_work(
        history, windows, slip_rate, loading, friction, state
    )

    outbound = call(
        lines_kernel,
        f32(1536, 128),
        [scratch(2, 1024, 128)],
        400_000_000,
        in_specs=[whole] * 3 + [remote],
    )(lines, twiddle(16, NY, -1), dft_matrix(-1, 1.0 / math.sqrt(NY), True), waves)
    arrived = lax.all_to_all(
        outbound.reshape(128, 12 * 128), everyone, split_axis=0, concat_axis=0, tiled=True
    ).reshape(1536, 128)
    spectrum, outgoing = call(
        modes_kernel,
        [f32(2, 16, NX), f32(1024, 128)],
        [
            scratch(768, 256),
            scratch(768, 256),
            scratch(2, 32, 8, 128),
            scratch(2, 8, NX),
            scratch(2, 16, NX),
            scratch(2, 512, 128),
            pltpu.SemaphoreType.DMA,
        ],
        600_000_000,
        in_specs=[whole] * 8,
        out_specs=[remote, whole],
    )(
        arrived,
        summed,
        waves,
        twiddle(32, NX, -1),
        twiddle(32, NX, 1),
        dft_matrix(-1, 1.0 / math.sqrt(NX), False),
        dft_matrix(1, 1.0 / math.sqrt(NX), False),
        constant_waves(),
    )
    returned = lax.all_to_all(
        outgoing.reshape(128, 8, 128), everyone, split_axis=0, concat_axis=0, tiled=True
    ).reshape(1024, 128)
    stress = call(cells_kernel, f32(16, 32, 128), [scratch(512, 256)], 200_000_000)(
        returned, twiddle(16, NY, 1), dft_matrix(1, 0.5 / math.sqrt(NY), False)
    )
    transfer = lax.all_to_all(stress, "cols", split_axis=0, concat_axis=0, tiled=True)
    transfer = transfer.reshape(512, 128)

    traction = loading + transfer
    half_gain = 0.5 * jnp.exp(state)
    steepness = friction * half_gain
    velocity = slip_rate - (start - transfer) * inverse
    for sweep in range(NEWTON - 1):
        scaled = velocity * half_gain
        square = 1.0 + scaled * scaled
        root = square * lax.rsqrt(square)
        magnitude = jnp.log(jnp.abs(scaled) + root)
        mismatch = friction * jnp.where(scaled < 0, -magnitude, magnitude) + damping * velocity - traction
        velocity = velocity - mismatch * root / (steepness + damping * root)
    return (velocity, traction - damping * velocity, spectrum)


def solution(mesh):
    cell = P("rows", "cols")
    placed = (cell,) * 5 + (P(None, None, ("rows", "cols"), None), P(("rows", "cols"), None))
    return jax.shard_map(
        on_device,
        mesh=mesh,
        in_specs=placed,
        out_specs=(cell, cell, P(None, ("rows", "cols"), None)),
        check_vma=False,
    )
```

```python
import functools
import math

import jax
import jax.numpy as jnp
import ml_dtypes
import numpy as np
from jax import lax
from jax.experimental import pallas as pl
from jax.experimental.pallas import tpu as pltpu
from jax.sharding import PartitionSpec as P

NX = 4096
NY = 2048
HIST = 32
NEWTON = 3
damping = 1.0
LANES = 512
LAGS = 4
VMEM_LIMIT = 24 * 1024 * 1024


def split_host(matrix):
    full = matrix.astype(np.float32)
    high = full.astype(ml_dtypes.bfloat16)
    low = (full - high.astype(np.float32)).astype(ml_dtypes.bfloat16)
    return np.stack((high, low))


def dft_matrix(sign, scale, transposed):
    index = np.arange(128)
    phase = sign * 2.0 * math.pi * (np.outer(index, index) % 128) / 128.0
    cos, sin = np.cos(phase) * scale, np.sin(phase) * scale
    matrix = np.block([[cos, sin], [-sin, cos]])
    return split_host(matrix.T if transposed else matrix)


def twiddle(count, length, sign):
    phase = sign * 2.0 * math.pi * np.outer(np.arange(count), np.arange(128)) / length
    return np.stack((np.cos(phase), np.sin(phase))).astype(np.float32)


def constant_waves():
    kx = np.arange(NX, dtype=np.float32)
    fold = np.minimum(kx, NX - kx) * np.float32(2.0 / NX)
    return fold.reshape(32, 128)


def add(a, b):
    return (a[0] + b[0], a[1] + b[1])


def sub(a, b):
    return (a[0] - b[0], a[1] - b[1])


def conj(a):
    return (a[0], -a[1])


def turn(value, numerator, length, sign):
    numerator %= length
    re, im = value
    if numerator == 0:
        return value
    if 4 * numerator == length:
        return (-im, re) if sign > 0 else (im, -re)
    if 2 * numerator == length:
        return (-re, -im)
    if 4 * numerator == 3 * length:
        return (im, -re) if sign > 0 else (-im, re)
    if 8 * numerator % length == 0:
        half = math.sqrt(0.5)
        octant = 8 * numerator // length
        cos_sign = 1.0 if octant in (1, 7) else -1.0
        sin_sign = (1.0 if octant in (1, 3) else -1.0) * sign
        first = re if cos_sign > 0 else -re
        second = im if cos_sign > 0 else -im
        if sin_sign > 0:
            return ((first - im) * half, (re + second) * half)
        return ((first + im) * half, (second - re) * half)
    angle = 2.0 * math.pi * numerator / length
    cos, sin = math.cos(angle), sign * math.sin(angle)
    return (re * cos - im * sin, re * sin + im * cos)


def butterfly(values, sign):
    size = len(values)
    if size == 1:
        return values
    even = butterfly(values[0::2], sign)
    odd = butterfly(values[1::2], sign)
    turned = [turn(odd[k], k, size, sign) for k in range(size // 2)]
    return [add(e, t) for e, t in zip(even, turned)] + [sub(e, t) for e, t in zip(even, turned)]


def real_forward(values):
    size = len(values)
    if size == 2:
        return [(values[0] + values[1], None), (values[0] - values[1], None)]
    even = real_forward(values[0::2])
    odd = real_forward(values[1::2])
    quarter = size // 4
    out = [None] * (size // 2 + 1)
    for k in range(quarter + 1):
        e, o = even[k], odd[k]
        if k == 0:
            out[0] = (e[0] + o[0], None)
            out[size // 2] = (e[0] - o[0], None)
        elif k == quarter:
            out[k] = (e[0], -o[0])
        else:
            t = turn(o, k, size, -1)
            out[k] = add(e, t)
            out[size // 2 - k] = conj(sub(e, t))
    return out


def real_inverse(modes):
    half = len(modes) - 1
    size = 2 * half
    if size == 2:
        return [modes[0][0] + modes[1][0], modes[0][0] - modes[1][0]]
    quarter = half // 2
    even, odd = [], []
    for k in range(quarter + 1):
        a, b = modes[k], modes[half - k]
        if k == 0:
            even.append((a[0] + b[0], None))
            odd.append((a[0] - b[0], None))
        elif k == quarter:
            even.append((a[0] + a[0], None))
            odd.append((-(a[1] + a[1]), None))
        else:
            even.append(add(a, conj(b)))
            odd.append(turn(sub(a, conj(b)), k, size, 1))
    first, second = real_inverse(even), real_inverse(odd)
    out = []
    for e, o in zip(first, second):
        out += [e, o]
    return out


def times(value, table, index, rows=None):
    cos, sin = table[0, index : index + 1, :], table[1, index : index + 1, :]
    re, im = value
    if im is None:
        return (re * cos, re * sin)
    return (re * cos - im * sin, re * sin + im * cos)


def first_wavenumber():
    return lax.axis_index(("rows", "cols")) * 16


def split(value):
    high = value.astype(jnp.bfloat16)
    return high, (value - high.astype(jnp.float32)).astype(jnp.bfloat16)


def dot(left, right):
    return jnp.dot(left, right, preferred_element_type=jnp.float32)


def dot_transposed(left, right):
    return lax.dot_general(
        left, right, (((1,), (1,)), ((), ())), preferred_element_type=jnp.float32
    )


def exact_dot(data, matrix):
    (high, low), (matrix_high, matrix_low) = data, matrix
    count = matrix_high.shape[1]
    wide = dot(high, jnp.concatenate((matrix_high, matrix_low), axis=1))
    return wide[:, :count] + (wide[:, count:] + dot(low, matrix_high))


def gather_kernel(slip, slip_rate, cells, held, sems):
    fields = (slip, slip_rate)
    reads = [pltpu.make_async_copy(fields[f], held.at[f], sems.at[f]) for f in range(2)]
    writes = [pltpu.make_async_copy(held.at[f], cells.at[:, f], sems.at[2 + f]) for f in range(2)]
    for read in reads:
        read.start()
    for read, write in zip(reads, writes):
        read.wait()
        write.start()
    for write in writes:
        write.wait()


def lines_kernel(cells, table, matrix, unused, out, work):
    del unused
    for f in range(2):
        for group in range(4):
            samples = [cells[c, f, 8 * group : 8 * group + 8, :] for c in range(16)]
            modes = real_forward(samples)
            for k in range(16 if f == 1 else 9):
                value = times(modes[k] if k <= 8 else conj(modes[16 - k]), table, k)
                if f == 1:
                    places = [pl.ds(group * 128 + k, 8, stride=16)]
                elif k < 8:
                    places = [pl.ds(512 + group * 64 + k, 8, stride=8)]
                else:
                    places = [pl.ds(768 + group * 64 + slot, 8, stride=8) for slot in range(8)]
                for rows in places:
                    work[0, rows, :] = value[0]
                    work[1, rows, :] = value[1]
    weights = (matrix[0], matrix[1])

    def transform(chunk):
        rows = pl.ds(chunk * 256, 256)
        turned = jnp.concatenate((work[0, rows, :], work[1, rows, :]), axis=1)
        high, low = split(turned)
        return dot_transposed(weights[0], high) + (
            dot_transposed(weights[1], high) + dot_transposed(weights[0], low)
        )

    def tile_of(result, part, piece):
        return result[part * 128 : part * 128 + 128, piece * 128 : piece * 128 + 128]

    for chunk in range(2):
        result = transform(chunk)
        for part in range(2):
            for piece in range(2):
                out[pl.ds(part * 4 + chunk * 2 + piece, 128, stride=12), :] = tile_of(
                    result, part, piece
                )
    lower, upper = transform(2), transform(3)
    owner = lax.broadcasted_iota(jnp.int32, (128, 128), 0)
    first_slot = lax.broadcasted_iota(jnp.int32, (128, 128), 1) % 8 == 0
    for part in range(2):
        for piece in range(2):
            tile = jnp.where(
                first_slot & (owner < 64), tile_of(upper, part, piece), tile_of(lower, part, piece)
            )
            if part == 1:
                constant = lower[0:1, piece * 128 : piece * 128 + 128]
                tile = jnp.where(first_slot & (owner == 64), constant, tile)
            out[pl.ds(8 + part * 2 + piece, 128, stride=12), :] = tile


def early_kernel(
    history, counts, rate, loading, friction, state, total, waves, start, inverse, stored, windows, cells, cosines, previous, sems
):
    groups = HIST // LAGS
    copies = [pltpu.make_async_copy(counts, windows, sems.at[groups])]
    for group in range(groups):
        lags = pl.ds(group * LAGS, LAGS)
        copies.append(pltpu.make_async_copy(history.at[lags], stored.at[lags], sems.at[group]))
    for index, field in enumerate((rate, loading, friction, state)):
        copies.append(pltpu.make_async_copy(field, cells.at[index], sems.at[groups + 1 + index]))
    for copy in copies:
        copy.start()
    shape = (16, LANES)

    @pl.loop(0, NX // LANES)
    def _(block):
        lanes = pl.ds(pl.multiple_of(block * LANES, LANES), LANES)
        ky = lax.broadcasted_iota(jnp.int32, shape, 0) + first_wavenumber()
        kx = lax.broadcasted_iota(jnp.int32, shape, 1) + block * LANES
        fold_x = jnp.minimum(kx, NX - kx).astype(jnp.float32) * (2.0 / NX)
        fold_y = jnp.minimum(ky, NY - ky).astype(jnp.float32) * (2.0 / NY)
        wave = jnp.sqrt(fold_x * fold_x + fold_y * fold_y)
        waves[:, lanes] = wave
        cosines[1, :, lanes] = jnp.cos(3.0 * wave)

    copies[0].wait()
    for group in range(groups):
        copies[group + 1].wait()

        @pl.loop(0, NX // LANES)
        def _(block):
            lanes = pl.ds(pl.multiple_of(block * LANES, LANES), LANES)
            now = cosines[1, :, lanes]
            double = now + now
            if group == 0:
                cosines[0, :, lanes] = double
                before = jnp.ones(shape, jnp.float32)
                real = jnp.zeros(shape, jnp.float32)
                imag = jnp.zeros(shape, jnp.float32)
            else:
                double = cosines[0, :, lanes]
                before = previous[:, lanes]
                real = total[0, :, lanes]
                imag = total[1, :, lanes]
            count = windows[:, lanes]
            for lag in range(group * LAGS + 1, group * LAGS + LAGS + 1):
                if lag > 1:
                    before, now = now, double * now - before
                weight = jnp.where(count >= lag, now * (2.0 * HIST + 2.0 - lag), 0.0)
                real = real + weight * stored[lag - 1, 0, :, lanes].astype(jnp.float32)
                imag = imag + weight * stored[lag - 1, 1, :, lanes].astype(jnp.float32)
            if group == groups - 1:
                factor = (waves[:, lanes] + 0.25) * (-0.5 / (2.0 * HIST + 2.0))
                real = real * factor
                imag = imag * factor
            else:
                cosines[1, :, lanes] = now
                previous[:, lanes] = before
            total[0, :, lanes] = real
            total[1, :, lanes] = imag

    for copy in copies[groups + 1 :]:
        copy.wait()

    @pl.loop(0, 8)
    def _(block):
        rows = pl.ds(pl.multiple_of(block * 64, 64), 64)
        velocity, strength = cells[0, rows, :], cells[2, rows, :]
        half_gain = 0.5 * jnp.exp(cells[3, rows, :])
        scaled = velocity * half_gain
        square = 1.0 + scaled * scaled
        root = square * lax.rsqrt(square)
        magnitude = jnp.log(jnp.abs(scaled) + root)
        stress = strength * jnp.where(scaled < 0, -magnitude, magnitude) + damping * velocity
        start[rows, :] = stress - cells[1, rows, :]
        inverse[rows, :] = root / (strength * half_gain + damping * root)


def modes_kernel(
    arrived,
    summed,
    waves,
    turn_in,
    turn_out,
    into,
    back,
    back_rows,
    constant_wave,
    spectrum_out,
    out,
    left,
    mid,
    spec,
    gathered,
    spectrum,
    turned,
    sem,
):
    for part in range(2):
        lanes = slice(part * 128, part * 128 + 128)
        for piece in range(4):
            tile = arrived[pl.ds(part * 4 + piece, 128, stride=12), :]
            left[piece * 128 : piece * 128 + 128, lanes] = tile.T
        for piece in range(2):
            tile = arrived[pl.ds(8 + part * 2 + piece, 128, stride=12), :]
            left[512 + piece * 128 : 640 + piece * 128, lanes] = tile.T
    weights = (into[0], into[1])
    for piece in range(3):
        rows = pl.ds(piece * 256, 256)
        mid[rows, :] = exact_dot(split(left[rows, :]), weights)
    for f, half, first, stride in [(1, 0, 0, 16), (1, 1, 8, 16), (0, 0, 512, 8)]:
        for i1 in range(4):
            values = []
            for i2 in range(8):
                i = i1 + 4 * i2
                rows = slice(first + i * stride, first + i * stride + 8)
                values.append(times((mid[rows, 0:128], mid[rows, 128:256]), turn_in, i))
            for b1, value in enumerate(butterfly(values, -1)):
                value = turn(value, i1 * b1, 32, -1)
                spec[0, i1 * 8 + b1] = value[0]
                spec[1, i1 * 8 + b1] = value[1]
        for b1 in range(8):
            values = [(spec[0, i1 * 8 + b1], spec[1, i1 * 8 + b1]) for i1 in range(4)]
            for b2, value in enumerate(butterfly(values, -1)):
                b = b1 + 8 * b2
                for part in range(2):
                    rows = slice(half * 8, half * 8 + 8)
                    lanes = slice(b * 128, b * 128 + 128)
                    if f == 1:
                        spectrum[part, rows, lanes] = value[part]
                    else:
                        gathered[part, :, lanes] = value[part]
        if f == 1 and half == 1:
            finished = pltpu.make_async_copy(spectrum, spectrum_out, sem)
            finished.start()
    sublane = lax.broadcasted_iota(jnp.int32, (8, 128), 0)
    first = first_wavenumber()
    share_zero = jnp.where(first == NY // 2, -0.5, jnp.where(first < NY // 2, 0.0, -1.0))
    share_eight = jnp.where(first < NY // 2, -1.0, 0.0)
    shares = (jnp.where(sublane == 0, share_zero, -1.0), jnp.where(sublane == 0, share_eight, 0.0))
    for half in range(2):
        rows = slice(half * 8, half * 8 + 8)
        for b1 in range(8):
            values = []
            for b2 in range(4):
                b = b1 + 8 * b2
                lanes = slice(b * 128, b * 128 + 128)
                wave = waves[rows, lanes]
                slip_weight = shares[half] * wave
                rate_weight = -0.5 * (wave + 0.25)
                values.append(
                    tuple(
                        slip_weight * gathered[part, :, lanes]
                        + rate_weight * spectrum[part, rows, lanes]
                        + summed[part, rows, lanes]
                        for part in range(2)
                    )
                )
            for i1, value in enumerate(butterfly(values, 1)):
                value = turn(value, i1 * b1, 32, 1)
                spec[0, i1 * 8 + b1] = value[0]
                spec[1, i1 * 8 + b1] = value[1]
        for i1 in range(4):
            values = [(spec[0, i1 * 8 + b1], spec[1, i1 * 8 + b1]) for b1 in range(8)]
            for i2, value in enumerate(butterfly(values, 1)):
                i = i1 + 4 * i2
                value = times(value, turn_out, i)
                start = (i // 8) * 128 + half * 64 + i % 8
                for part in range(2):
                    turned[part, pl.ds(start, 8, stride=8), :] = value[part]
    weights = (back[0], back[1])

    def transform(rows, weights):
        lines = jnp.concatenate((turned[0, rows, :], turned[1, rows, :]), axis=1)
        return exact_dot(split(lines), weights)

    for chunk in range(2):
        rows = pl.ds(chunk * 256, 256)
        high, low = split(jnp.concatenate((turned[0, rows, :], turned[1, rows, :]), axis=1))
        result = dot_transposed(back_rows[0], high) + (
            dot_transposed(back_rows[1], high) + dot_transposed(back_rows[0], low)
        )
        for part in range(2):
            for piece in range(2):
                tile = result[part * 128 : part * 128 + 128, piece * 128 : piece * 128 + 128]
                group = chunk * 2 + piece
                out[pl.ds(part * 4 + group, 128, stride=8), :] = tile

    @pl.when(first == NY // 2)
    def _():
        for b1 in range(8):
            values = []
            for b2 in range(4):
                b = b1 + 8 * b2
                weight = constant_wave[b : b + 1, :] * -0.5
                values.append(
                    tuple(
                        jnp.broadcast_to(
                            gathered[part, 0:1, b * 128 : b * 128 + 128] * weight, (8, 128)
                        )
                        for part in range(2)
                    )
                )
            for i1, value in enumerate(butterfly(values, 1)):
                value = turn(value, i1 * b1, 32, 1)
                spec[0, i1 * 8 + b1] = value[0]
                spec[1, i1 * 8 + b1] = value[1]
        for i1 in range(4):
            values = [(spec[0, i1 * 8 + b1], spec[1, i1 * 8 + b1]) for b1 in range(8)]
            for i2, value in enumerate(butterfly(values, 1)):
                i = i1 + 4 * i2
                value = times(value, turn_out, i)
                for part in range(2):
                    turned[part, i : i + 1, :] = value[part][0:1, :]
        constant = transform(pl.ds(0, 128), (back[0, :, 128:256], back[1, :, 128:256])).T
        lane = lax.broadcasted_iota(jnp.int32, (128, 128), 1)
        for group in range(4):
            rows = pl.ds(4 + group, 128, stride=8)
            moved = pltpu.roll(constant, (128 - 8 * group) % 128, 1)
            out[rows, :] = jnp.where(lane < 8, moved, out[rows, :])

    finished.wait()


def cells_kernel(arrived, table, matrix, out, left):
    for piece in range(4):
        for part in range(2):
            tile = arrived[pl.ds(part * 4 + piece, 128, stride=8), :]
            left[piece * 128 : piece * 128 + 128, part * 128 : part * 128 + 128] = tile.T
    means = [left[piece * 128 : piece * 128 + 8, 192:193] for piece in range(4)]
    weights = (matrix[0], matrix[1])
    for chunk in range(2):
        rows = pl.ds(chunk * 256, 256)
        left[rows, :] = exact_dot(split(left[rows, :]), weights)
    for piece in range(4):
        values = []
        for k in range(16):
            row = piece * 128 + k * 8
            value = (left[row : row + 8, 0:128], left[row : row + 8, 128:256])
            values.append(times(value, table, k))
        constant = values[0][0] + means[piece] * (0.5 / math.sqrt(NY))
        modes = [(constant + constant, None)]
        modes += [add(values[k], conj(values[16 - k])) for k in range(1, 8)]
        modes += [(values[8][0] + values[8][0], None)]
        for c, value in enumerate(real_inverse(modes)):
            out[c, piece * 8 : piece * 8 + 8, :] = value


def call(kernel, out_shape, scratch, flops, **extra):
    return pl.pallas_call(
        kernel,
        out_shape=out_shape,
        scratch_shapes=scratch,
        compiler_params=pltpu.CompilerParams(vmem_limit_bytes=VMEM_LIMIT),
        cost_estimate=pl.CostEstimate(flops=flops, bytes_accessed=4 << 20, transcendentals=0),
        **extra,
    )


def f32(*shape):
    return jax.ShapeDtypeStruct(shape, jnp.float32)


def early_work(*arrays):
    return pl.pallas_call(
        early_kernel,
        in_specs=[pl.BlockSpec(memory_space=pl.ANY)] * 6,
        out_shape=[f32(2, 16, NX), f32(16, NX), f32(512, 128), f32(512, 128)],
        scratch_shapes=[
            pltpu.VMEM((HIST, 2, 16, NX), jnp.bfloat16),
            pltpu.VMEM((16, NX), jnp.int32),
            pltpu.VMEM((4, 512, 128), jnp.float32),
            pltpu.VMEM((2, 16, NX), jnp.float32),
            pltpu.VMEM((16, NX), jnp.float32),
            pltpu.SemaphoreType.DMA((HIST // LAGS + 5,)),
        ],
        compiler_params=pltpu.CompilerParams(vmem_limit_bytes=VMEM_LIMIT),
        cost_estimate=pl.CostEstimate(
            flops=40_000_000, bytes_accessed=10 << 20, transcendentals=3 * 65536
        ),
    )(*(pltpu.with_memory_space_constraint(array, pltpu.HBM) for array in arrays))


def on_device(slip, slip_rate, loading, friction, state, history, windows):
    everyone = ("rows", "cols")
    scratch = lambda *shape: pltpu.VMEM(shape, jnp.float32)
    whole = pl.BlockSpec(memory_space=pltpu.VMEM)
    remote = pl.BlockSpec(memory_space=pl.ANY)
    remote = pl.BlockSpec(memory_space=pl.ANY)
    cells = pl.pallas_call(
        gather_kernel,
        in_specs=[remote] * 2,
        out_specs=remote,
        out_shape=pltpu.HBM((16, 2, 32, 128), jnp.float32),
        scratch_shapes=[
            pltpu.VMEM((2, 16, 32, 128), jnp.float32),
            pltpu.SemaphoreType.DMA((4,)),
        ],
    )(
        pltpu.with_memory_space_constraint(slip.reshape(16, 32, 128), pltpu.HBM),
        pltpu.with_memory_space_constraint(slip_rate.reshape(16, 32, 128), pltpu.HBM),
    )
    lines = lax.all_to_all(cells, "cols", split_axis=0, concat_axis=0, tiled=True)

    summed, waves, start, inverse = early_work(
        history, windows, slip_rate, loading, friction, state
    )

    outbound = call(
        lines_kernel,
        f32(1536, 128),
        [scratch(2, 1024, 128)],
        400_000_000,
        in_specs=[whole] * 3 + [remote],
    )(lines, twiddle(16, NY, -1), dft_matrix(-1, 1.0 / math.sqrt(NY), True), waves)
    arrived = lax.all_to_all(
        outbound.reshape(128, 12 * 128), everyone, split_axis=0, concat_axis=0, tiled=True
    ).reshape(1536, 128)
    spectrum, outgoing = call(
        modes_kernel,
        [f32(2, 16, NX), f32(1024, 128)],
        [
            scratch(768, 256),
            scratch(768, 256),
            scratch(2, 32, 8, 128),
            scratch(2, 8, NX),
            scratch(2, 16, NX),
            scratch(2, 512, 128),
            pltpu.SemaphoreType.DMA,
        ],
        600_000_000,
        in_specs=[whole] * 9,
        out_specs=[remote, whole],
    )(
        arrived,
        summed,
        waves,
        twiddle(32, NX, -1),
        twiddle(32, NX, 1),
        dft_matrix(-1, 1.0 / math.sqrt(NX), False),
        dft_matrix(1, 1.0 / math.sqrt(NX), False),
        dft_matrix(1, 1.0 / math.sqrt(NX), True),
        constant_waves(),
    )
    returned = lax.all_to_all(
        outgoing.reshape(128, 8, 128), everyone, split_axis=0, concat_axis=0, tiled=True
    ).reshape(1024, 128)
    stress = call(cells_kernel, f32(16, 32, 128), [scratch(512, 256)], 200_000_000)(
        returned, twiddle(16, NY, 1), dft_matrix(1, 0.5 / math.sqrt(NY), False)
    )
    transfer = lax.all_to_all(stress, "cols", split_axis=0, concat_axis=0, tiled=True)
    transfer = transfer.reshape(512, 128)

    traction = loading + transfer
    half_gain = 0.5 * jnp.exp(state)
    steepness = friction * half_gain
    velocity = slip_rate - (start - transfer) * inverse
    for sweep in range(NEWTON - 1):
        scaled = velocity * half_gain
        square = 1.0 + scaled * scaled
        root = square * lax.rsqrt(square)
        magnitude = jnp.log(jnp.abs(scaled) + root)
        mismatch = friction * jnp.where(scaled < 0, -magnitude, magnitude) + damping * velocity - traction
        velocity = velocity - mismatch * root / (steepness + damping * root)
    return (velocity, traction - damping * velocity, spectrum)


def solution(mesh):
    cell = P("rows", "cols")
    placed = (cell,) * 5 + (P(None, None, ("rows", "cols"), None), P(("rows", "cols"), None))
    return jax.shard_map(
        on_device,
        mesh=mesh,
        in_specs=placed,
        out_specs=(cell, cell, P(None, ("rows", "cols"), None)),
        check_vma=False,
    )
```
